32 devices in a mesh: gx: 8 (over y, x, core), gy: 4 (over z).
Axes of the slice: x: 2, y: 2, z: 4, core: 2. Of those that a mesh axis runs over, the one named last changes fastest.
Arguments:
- features: bfloat16 [8, 4, 4, 6144], P('gx', 'gy'), may hold values from -6 to 6
- cotangent: bfloat16 [8, 4, 4, 6144], P('gx', 'gy'), may hold values from -6 to 6
- brick_slot: int32 [8, 4, 2, 2, 2], P('gx', 'gy'), may hold values from 0 to 4, as said below
- weight_one: bfloat16 [27, 96, 96], replicated, may hold values from -0.125 to 0.125
- weight_two: bfloat16 [27, 96, 96], replicated, may hold values from -0.125 to 0.125
- gain: float32 [96], replicated, may hold values from 0.1 to 1.9
- bias: float32 [96], replicated, may hold values from -0.5 to 0.5
Outputs:
- out: bfloat16 [8, 4, 4, 6144], P('gx', 'gy')
- grad_features: bfloat16 [8, 4, 4, 6144], P('gx', 'gy')
- grad_weight_one: float32 [27, 96, 96], replicated
- grad_weight_two: float32 [27, 96, 96], replicated
- grad_gain: float32 [96], replicated
- grad_bias: float32 [96], replicated
The draws below stay inside these ranges and needn't reach their ends.
Inputs may be any that keep to these rules, and one draw needn't show every extreme that they name: `brick_slot`: on each slab the values below 4 are the slots 0 to n - 1, each in exactly one cell, for some n from 2 to 4; all other cells hold 4. At least one slab has n = 4.
All inputs are finite; a program needn't handle non-finite values.
Results may differ from the reference program's by a relative error of at most 0.003.
Values may be sent and summed in bfloat16 or wider, within the bound.
A program may use at most 64 MiB of HBM per device.

```python
import math
import jax
import jax.numpy as jnp
from jax import lax

C = 96
TAPS = 27
VOX = 64
BSIDE = 2
COLUMN = 2
CELLS = 8
NB = 4
SLABS_X = 8
SLABS_Y = 4


def draw_brick_slot(key, part):
    devices = SLABS_X * SLABS_Y
    key_count = jax.random.fold_in(key, 11)
    key_full = jax.random.fold_in(key, 23)
    key_order = jax.random.fold_in(key, 37)
    counts = jax.random.randint(key_count, (devices,), NB // 2, NB + 1)
    chosen = jax.random.randint(key_full, (), 0, devices)
    counts = jnp.where(jnp.arange(devices) == chosen, NB, counts)
    orders = jax.vmap(lambda one_key: jax.random.permutation(one_key, CELLS))(jax.random.split(key_order, devices))
    ranks = jnp.argsort(orders, axis=1)
    slots = jnp.where(ranks < counts[:, None], ranks, NB)
    return slots.reshape(SLABS_X, SLABS_Y, BSIDE, BSIDE, COLUMN).astype(jnp.int32)


def block_levels(own_key, extent, cuts, smallest, largest):
    def one(position, shards_of):
        steps = jax.random.uniform(jax.random.fold_in(jax.random.fold_in(own_key, 6), position), (shards_of,), jnp.float32, smallest / len(cuts), largest / len(cuts))
        return jnp.repeat(jnp.exp(steps), extent[position] // shards_of).reshape((-1,) + (1,) * (len(extent) - position - 1))

    level = one(*cuts[0])
    for cut in cuts[1:]:
        level = level * one(*cut)
    return level


def noise(rng, extent, scale, most, cuts=(), held_as=jnp.bfloat16):
    values = scale * jax.random.normal(rng, extent, jnp.float32)
    if cuts:
        values = values * block_levels(rng, extent, cuts, -0.22, 0.18)
    return jnp.clip(values, -most, most).astype(held_as)


def setup_inputs(seed: int = 0) -> dict:
    splits = jax.random.split(jax.random.key(seed), 8)
    return {
        "features": noise(splits[0], (SLABS_X, SLABS_Y, NB, VOX * C), 1.0, 6.0, ((0, 8), (1, 4))),
        "cotangent": noise(splits[1], (SLABS_X, SLABS_Y, NB, VOX * C), 1.0, 6.0, ((0, 8), (1, 4))),
        "brick_slot": draw_brick_slot(jax.random.fold_in(splits[7], 71), 0),
        "weight_one": noise(splits[3], (TAPS, C, C), (TAPS * C) ** -0.5, 0.125),
        "weight_two": noise(splits[4], (TAPS, C, C), (TAPS * C) ** -0.5, 0.125),
        "gain": jnp.clip(1.0 + 0.18 * jax.random.normal(splits[5], (C,), jnp.float32), 0.1, 1.9),
        "bias": jnp.clip(jax.random.uniform(splits[6], (C,), jnp.float32, -0.5, 0.5), -0.5, 0.5),
    }


def brick_layout(slot_cells, count_slots, cells_side, column):
    total_cells = slot_cells.shape[0]
    cell_ids = jnp.zeros((count_slots + 1,), jnp.int32).at[slot_cells].set(jnp.arange(total_cells, dtype=jnp.int32))[:count_slots]
    filled = jnp.sum((slot_cells < count_slots).astype(jnp.int32))
    live = (jnp.arange(count_slots, dtype=jnp.int32) < filled).astype(jnp.float32)
    cell_x = cell_ids // (cells_side * column)
    cell_y = cell_ids // column % cells_side
    cell_z = cell_ids % column
    return ((cell_x, cell_y, cell_z), live)

def assemble(ext_flat, cells, span_y, span_z):
    pieces_at = {-1: slice(3, 4), 0: slice(0, 4), 1: slice(0, 1)}
    planes = []
    for along_x in (-1, 0, 1):
        lines = []
        for along_y in (-1, 0, 1):
            blocks = []
            for along_z in (-1, 0, 1):
                rows_index = ((cells[0] + 1 + along_x) * span_y + cells[1] + 1 + along_y) * span_z + cells[2] + 1 + along_z
                whole_bricks = jnp.take(ext_flat, rows_index, axis=0)
                blocks.append(whole_bricks[:, pieces_at[along_x], pieces_at[along_y], pieces_at[along_z], :])
            lines.append(jnp.concatenate(blocks, axis=3))
        planes.append(jnp.concatenate(lines, axis=2))
    return jnp.concatenate(planes, axis=1)

def conv_taps(padded, kernel):
    channels = kernel.shape[1]
    total = jnp.zeros((padded.shape[0] * 64, channels), jnp.float32)
    for along_x in (-1, 0, 1):
        for along_y in (-1, 0, 1):
            for along_z in (-1, 0, 1):
                tap = 9 * (along_x + 1) + 3 * (along_y + 1) + (along_z + 1)
                window = padded[:, 1 + along_x:5 + along_x, 1 + along_y:5 + along_y, 1 + along_z:5 + along_z, :]
                total = total + jnp.dot(window.reshape(-1, channels), kernel[tap], preferred_element_type=jnp.float32)
    return total.reshape(padded.shape[0], 4, 4, 4, channels)

def weight_taps(padded, grads):
    channels = grads.shape[-1]
    flat_grads = grads.reshape(-1, channels)
    results = []
    for along_x in (-1, 0, 1):
        for along_y in (-1, 0, 1):
            for along_z in (-1, 0, 1):
                window = padded[:, 1 + along_x:5 + along_x, 1 + along_y:5 + along_y, 1 + along_z:5 + along_z, :]
                results.append(jnp.dot(window.reshape(-1, channels).T, flat_grads, preferred_element_type=jnp.float32))
    return jnp.stack(results, axis=0)

def flipped(kernel):
    return jnp.transpose(jnp.flip(kernel, 0), (0, 2, 1))

def reference(features, cotangent, brick_slot, weight_one, weight_two, gain, bias):
    devices = SLABS_X * SLABS_Y
    width = VOX * C
    slot_all = brick_slot.reshape(devices, CELLS)

    def global_grid(values):
        source = jnp.concatenate([values, jnp.zeros((devices, 1, width), values.dtype)], axis=1)
        grids = jax.vmap(lambda source_rows, cell_picks: jnp.take(source_rows, cell_picks, axis=0))(source, slot_all)
        grids = grids.reshape(SLABS_X, SLABS_Y, BSIDE, BSIDE, COLUMN, width)
        grids = grids.transpose(0, 2, 1, 3, 4, 5).reshape(SLABS_X * BSIDE, SLABS_Y * BSIDE, COLUMN, width)
        return jnp.pad(grids, ((1, 1), (1, 1), (1, 1), (0, 0)))

    def padded_at(whole, device):
        start_x = device // SLABS_Y * BSIDE
        start_y = device % SLABS_Y * BSIDE
        extended = lax.dynamic_slice(whole, (start_x, start_y, device * 0, device * 0), (BSIDE + 2, BSIDE + 2, COLUMN + 2, width))
        ext_flat = extended.reshape(-1, 4, 4, 4, C)
        cells, live = brick_layout(slot_all[device], NB, BSIDE, COLUMN)
        return (assemble(ext_flat, cells, BSIDE + 2, COLUMN + 2), live)

    def conv_all(values, kernel):
        whole = global_grid(values.reshape(devices, NB, width))

        def one_slab(device):
            padded, live = padded_at(whole, device)
            return conv_taps(padded, kernel) * live[:, None, None, None, None]
        return lax.map(one_slab, jnp.arange(devices, dtype=jnp.int32))

    def grads_all(values, grads):
        whole = global_grid(values.reshape(devices, NB, width))

        def add_slab(total, device):
            padded, live = padded_at(whole, device)
            return (total + weight_taps(padded, grads[device]), None)
        start = jnp.zeros((TAPS, C, C), jnp.float32)
        return lax.scan(add_slab, start, jnp.arange(devices, dtype=jnp.int32))[0]
    live_all = jax.vmap(lambda slot_cells: brick_layout(slot_cells, NB, BSIDE, COLUMN)[1])(slot_all)
    live_all = live_all[:, :, None, None, None, None]
    inputs = features.reshape(devices, NB, 4, 4, 4, C)
    upstream = cotangent.reshape(devices, NB, 4, 4, 4, C)
    first_conv = conv_all(inputs, weight_one)
    pre = first_conv * gain + bias
    hidden = (jax.nn.silu(pre) * live_all).astype(jnp.bfloat16)
    out = ((inputs.astype(jnp.float32) + conv_all(hidden, weight_two)) * live_all).astype(jnp.bfloat16)
    masked_cotangent = (upstream.astype(jnp.float32) * live_all).astype(jnp.bfloat16)
    grad_two = grads_all(hidden, masked_cotangent)
    back_hidden = conv_all(masked_cotangent, flipped(weight_two))
    sigmoid = jax.nn.sigmoid(pre)
    back_pre = back_hidden * (sigmoid * (1.0 + pre * (1.0 - sigmoid)))
    grad_gain = lax.optimization_barrier(jnp.sum(back_pre * first_conv, axis=(0, 1, 2, 3, 4)))
    grad_bias = lax.optimization_barrier(jnp.sum(back_pre, axis=(0, 1, 2, 3, 4)))
    back_conv = (back_pre * gain).astype(jnp.bfloat16)
    grad_one = grads_all(inputs, back_conv)
    grad_features = ((upstream.astype(jnp.float32) + conv_all(back_conv, flipped(weight_one))) * live_all).astype(jnp.bfloat16)
    scale = 1.0 / math.sqrt(devices * NB * VOX)
    return (out.reshape(SLABS_X, SLABS_Y, NB, width), grad_features.reshape(SLABS_X, SLABS_Y, NB, width), grad_one * scale, grad_two * scale, grad_gain * scale, grad_bias * scale)
```

```python
import functools
import math

import jax
import jax.numpy as jnp
from jax import lax
from jax.experimental import pallas as pl
from jax.experimental.pallas import tpu as pltpu
from jax.sharding import PartitionSpec as P

F32 = jnp.float32
BF16 = jnp.bfloat16
MESH = pl.DeviceIdType.MESH
LANES = 128
TAPS = 27
OFFSETS = (-1, 0, 1)
DIRECTIONS = tuple((i, j) for i in OFFSETS for j in OFFSETS if (i, j) != (0, 0))


def source_range(step):
    return pl.ds(1, 8) if step == 0 else pl.ds(8 if step > 0 else 1, 1)


def landing_range(step):
    return pl.ds(1, 8) if step == 0 else pl.ds(0 if step > 0 else 9, 1)


def bit_orders(size_x, size_y):
    bits_x = [("gx", 1 << i) for i in range(size_x.bit_length() - 1)]
    bits_y = [("gy", 1 << i) for i in range(size_y.bit_length() - 1)]
    first = bits_x + bits_y
    second = bits_x[:1] + bits_x[1:][::-1] + bits_y
    return first, second


def kernel(
    size_x, size_y, tiles, scale,
    slots, fields, w_one, w_two, gain_in, bias_in,
    out, grad_out, gw_one, gw_two, gg_out, gb_out,
    held, held_two, shifted, cols_a, cols_b, wm_one, wm_two, wt_one, wt_two, pad_rows,
    red_a, red_b, in_a, in_b, all_a, all_b,
    halo_send, halo_recv, sum_send, sum_recv,
):
    px, py = lax.axis_index("gx"), lax.axis_index("gy")
    orders = bit_orders(size_x, size_y)
    stages = len(orders[0])

    def exists(dx, dy):
        ok = None
        for pos, step, size in ((px, dx, size_x), (py, dy, size_y)):
            if step == 0:
                continue
            one = pos + step < size if step > 0 else pos >= 1
            ok = one if ok is None else jnp.logical_and(ok, one)
        return ok

    def at_step(dx, dy):
        return {"gx": px + dx, "gy": py + dy}

    def my_bit(axis, bit):
        return lax.rem((px if axis == "gx" else py) // bit, 2)

    def partner(axis, bit):
        move = (1 - 2 * my_bit(axis, bit)) * bit
        return at_step(move, 0) if axis == "gx" else at_step(0, move)

    held[...] = jnp.zeros_like(held)
    held_two[...] = jnp.zeros_like(held_two)

    barrier = pltpu.get_barrier_semaphore()
    greeted = jnp.int32(0)
    for dx, dy in DIRECTIONS:
        there = exists(dx, dy)
        greeted = greeted + jnp.where(there, 1, 0)

        @pl.when(there)
        def _(dx=dx, dy=dy):
            pl.semaphore_signal(barrier, inc=1, device_id=at_step(dx, dy), device_id_type=MESH)

    for axis, bit in orders[0]:
        pl.semaphore_signal(barrier, inc=1, device_id=partner(axis, bit), device_id_type=MESH)

    z_index = lax.broadcasted_iota(jnp.int32, (1, 8, LANES), 1)
    low_half = jnp.where(z_index < 4, 1.0, 0.0).astype(F32)
    high_half = 1.0 - low_half
    cell_slot = [slots[c] for c in range(8)]

    def picks(i, j, s):
        cell = (i * 2 + j) * 2
        lower = jnp.where(cell_slot[cell] == s, 1.0, 0.0).astype(F32)
        upper = jnp.where(cell_slot[cell + 1] == s, 1.0, 0.0).astype(F32)
        return lower * low_half + upper * high_half

    masks = {(i, j, s): picks(i, j, s) for i in range(2) for j in range(2) for s in range(4)}
    filled = {
        (i, j): masks[i, j, 0] + masks[i, j, 1] + masks[i, j, 2] + masks[i, j, 3]
        for i in range(2)
        for j in range(2)
    }
    for f in range(2):
        for i in range(2):
            for j in range(2):
                total = fields[f, 0] * masks[i, j, 0]
                for s in range(1, 4):
                    total = total + fields[f, s] * masks[i, j, s]
                held[f, 1 + 4 * i : 5 + 4 * i, 1 + 4 * j : 5 + 4 * j] = total.reshape(
                    4, 4, 8, LANES
                )

    pl.semaphore_wait(barrier, greeted + stages)

    def halo_copy(buf, phase, number):
        dx, dy = DIRECTIONS[number]
        return pltpu.make_async_remote_copy(
            src_ref=buf.at[:, source_range(dx), source_range(dy)],
            dst_ref=buf.at[:, landing_range(dx), landing_range(dy)],
            send_sem=halo_send.at[phase, number],
            recv_sem=halo_recv.at[phase, number],
            device_id=at_step(dx, dy),
            device_id_type=MESH,
        )

    def halo_start(buf, phase):
        for number, (dx, dy) in enumerate(DIRECTIONS):

            @pl.when(exists(dx, dy))
            def _(number=number):
                halo_copy(buf, phase, number).start()

    def halo_arrive(buf, phase):
        for number, (dx, dy) in enumerate(DIRECTIONS):

            @pl.when(exists(-dx, -dy))
            def _(number=number):
                halo_copy(buf, phase, number).wait_recv()

    def halo_sent(buf, phase):
        for number, (dx, dy) in enumerate(DIRECTIONS):

            @pl.when(exists(dx, dy))
            def _(number=number):
                halo_copy(buf, phase, number).wait_send()

    halo_start(held, 0)

    for w_in, wide, turned in ((w_one, wm_one, wt_one), (w_two, wm_two, wt_two)):
        wide[...] = jnp.zeros_like(wide)
        for t in range(TAPS):
            wide[t * LANES : t * LANES + 96, 0:96] = w_in[t]
        for t in range(TAPS):
            flip = (TAPS - 1 - t) * LANES
            turned[t * LANES : (t + 1) * LANES, :] = (
                wide[flip : flip + LANES, :].astype(F32).T.astype(BF16)
            )
    pad_rows[...] = jnp.zeros_like(pad_rows)
    pad_rows[0:1, 0:96] = gain_in[...]
    pad_rows[1:2, 0:96] = bias_in[...]
    gain = pad_rows[0:1, :]
    bias = pad_rows[1:2, :]
    red_a[...] = jnp.zeros_like(red_a)
    red_b[...] = jnp.zeros_like(red_b)

    def columns(buf, f, cols):
        values = buf[f].reshape(100, 8, LANES)
        shifted[1] = values.reshape(10, 10, 8, LANES)
        shifted[0] = jnp.where(z_index == 0, 0.0, pltpu.roll(values, 1, 1)).reshape(
            10, 10, 8, LANES
        )
        shifted[2] = jnp.where(z_index == 7, 0.0, pltpu.roll(values, 7, 1)).reshape(
            10, 10, 8, LANES
        )
        for t in range(TAPS):
            a, b, c = t // 9, t // 3 % 3, t % 3
            cols[:, t * LANES : (t + 1) * LANES] = (
                shifted[c, a : a + 8, b : b + 8].reshape(512, LANES).astype(BF16)
            )

    def dense_mask():
        rows = []
        for i in range(2):
            line = jnp.concatenate(
                [jnp.broadcast_to(filled[i, j], (4, 8, LANES)) for j in range(2)], axis=0
            )
            rows.append(jnp.broadcast_to(line[None], (4, 8, 8, LANES)))
        return jnp.concatenate(rows, axis=0).reshape(512, LANES)

    def interior(buf, f):
        return buf[f, 1:9, 1:9].reshape(512, LANES)

    def dot(lhs, rhs):
        return jnp.dot(lhs, rhs, preferred_element_type=F32)

    def weight_sums(left, cols, red):
        left_t = left.T.astype(BF16)[0:96]
        for t in range(TAPS):
            red[pl.ds((TAPS - 1 - t) * 12, 12)] = dot(
                left_t, cols[:, t * LANES : (t + 1) * LANES]
            ).reshape(12, 8, LANES)

    halo_arrive(held, 0)
    occupied = dense_mask()
    columns(held, 0, cols_a)
    first_conv = dot(cols_a[...], wm_one[...]) * occupied
    pre = first_conv * gain + bias
    sigmoid = 1.0 / (1.0 + jnp.exp(-pre))
    hidden = occupied * (pre * sigmoid)
    held_two[0, 1:9, 1:9] = hidden.reshape(8, 8, 8, LANES)
    columns(held, 1, cols_b)
    back_hidden = dot(cols_b[...], wt_two[...]) * occupied
    back_pre = back_hidden * (sigmoid * (1.0 + pre * (1.0 - sigmoid)))
    held_two[1, 1:9, 1:9] = (back_pre * gain).reshape(8, 8, 8, LANES)
    halo_start(held_two, 1)
    red_b[TAPS * 12, 0:1, :] = jnp.sum(back_pre * first_conv, axis=0, keepdims=True)
    red_b[TAPS * 12, 1:2, :] = jnp.sum(back_pre, axis=0, keepdims=True)

    reds, ins, alls = (red_a, red_b), (in_a, in_b), (all_a, all_b)
    offsets = ([jnp.int32(0)], [jnp.int32(0)])

    def half_of(stage):
        return tiles >> (stage + 1)

    def scatter_copy(which, stage):
        axis, bit = orders[which][stage]
        half = half_of(stage)
        give = offsets[which][stage] + (1 - my_bit(axis, bit)) * half
        return pltpu.make_async_remote_copy(
            src_ref=reds[which].at[pl.ds(give, half)],
            dst_ref=ins[which].at[pl.ds(tiles - 2 * half, half)],
            send_sem=sum_send.at[which, stage],
            recv_sem=sum_recv.at[which, stage],
            device_id=partner(axis, bit),
            device_id_type=MESH,
        )

    def gather_copy(which, stage):
        axis, bit = orders[which][stage]
        half = half_of(stage)
        keep = offsets[which][stage + 1]
        rows = alls[which].at[pl.ds(keep, half)]
        return pltpu.make_async_remote_copy(
            src_ref=rows,
            dst_ref=rows,
            send_sem=sum_send.at[which, 2 * stages - 1 - stage],
            recv_sem=sum_recv.at[which, 2 * stages - 1 - stage],
            device_id=partner(axis, bit),
            device_id_type=MESH,
        )

    def scatter_end(which, stage):
        axis, bit = orders[which][stage]
        half = half_of(stage)
        scatter_copy(which, stage).wait()
        keep = offsets[which][stage] + my_bit(axis, bit) * half
        offsets[which].append(keep)
        total = reds[which][pl.ds(keep, half)] + ins[which][pl.ds(tiles - 2 * half, half)]
        if stage == stages - 1:
            alls[which][pl.ds(keep, half)] = total * scale
        else:
            reds[which][pl.ds(keep, half)] = total

    def advance(which, step):
        if step > 0:
            if step <= stages:
                scatter_end(which, step - 1)
            else:
                gather_copy(which, 2 * stages - step).wait()
        if step < stages:
            scatter_copy(which, step).start()
        elif step < 2 * stages:
            gather_copy(which, 2 * stages - 1 - step).start()

    weight_sums(interior(held_two, 0), cols_b, red_a)
    advance(0, 0)
    halo_arrive(held_two, 1)
    columns(held_two, 1, cols_a)
    weight_sums(interior(held, 0), cols_a, red_b)
    advance(1, 0)
    advance(0, 1)

    def to_slots(dense, ref):
        dense = dense.reshape(8, 8, 8, LANES)
        for s in range(4):
            total = None
            for i in range(2):
                for j in range(2):
                    part = dense[4 * i : 4 * i + 4, 4 * j : 4 * j + 4].reshape(16, 8, LANES)
                    part = part * masks[i, j, s]
                    total = part if total is None else total + part
            ref[s] = total + pltpu.roll(total, 4, 1)

    to_slots(interior(held, 1) + dot(cols_a[...], wt_one[...]), grad_out)
    advance(1, 1)
    columns(held_two, 0, cols_b)
    advance(0, 2)
    to_slots(interior(held, 0) + dot(cols_b[...], wm_two[...]), out)
    for step in range(2, 2 * stages + 1):
        advance(1, step)
        if step < 2 * stages:
            advance(0, step + 1)

    for t in range(TAPS):
        rows = pl.ds(t * 12, 12)
        gw_two[t] = all_a[rows].reshape(96, LANES)[:, 0:96]
        gw_one[t] = all_b[rows].reshape(96, LANES)[:, 0:96]
    gg_out[...] = all_b[TAPS * 12, 0:1, 0:96]
    gb_out[...] = all_b[TAPS * 12, 1:2, 0:96]
    halo_sent(held, 0)
    halo_sent(held_two, 1)


def body(features, cotangent, brick_slot, weight_one, weight_two, gain, bias):
    count_slots = features.shape[2]
    channels = gain.shape[0]
    size_x, size_y = lax.axis_size("gx"), lax.axis_size("gy")
    devices = size_x * size_y
    scale = 1.0 / math.sqrt(devices * count_slots * 64)
    tiles = -(-(TAPS * 12 + 1) // devices) * devices
    stages = (devices).bit_length() - 1
    fields = jnp.stack([features, cotangent]).reshape(2, count_slots, 16, 4, channels)
    fields = jnp.concatenate([fields, fields], axis=3).astype(F32)
    fields = jnp.pad(fields, ((0, 0), (0, 0), (0, 0), (0, 0), (0, LANES - channels)))
    vmem = pl.BlockSpec(memory_space=pltpu.VMEM)
    smem = pl.BlockSpec(memory_space=pltpu.SMEM)
    slot_shape = jax.ShapeDtypeStruct((count_slots, 16, 8, LANES), F32)
    weight_shape = jax.ShapeDtypeStruct((TAPS, channels, channels), F32)
    row_shape = jax.ShapeDtypeStruct((1, channels), F32)
    out, grad_features, gw_one, gw_two, gg, gb = pl.pallas_call(
        functools.partial(kernel, size_x, size_y, tiles, scale),
        out_shape=(slot_shape, slot_shape, weight_shape, weight_shape, row_shape, row_shape),
        in_specs=[smem] + [vmem] * 5,
        out_specs=(vmem,) * 6,
        scratch_shapes=[
            pltpu.VMEM((2, 10, 10, 8, LANES), F32),
            pltpu.VMEM((2, 10, 10, 8, LANES), F32),
            pltpu.VMEM((3, 10, 10, 8, LANES), F32),
            pltpu.VMEM((512, TAPS * LANES), BF16),
            pltpu.VMEM((512, TAPS * LANES), BF16),
            pltpu.VMEM((TAPS * LANES, LANES), BF16),
            pltpu.VMEM((TAPS * LANES, LANES), BF16),
            pltpu.VMEM((TAPS * LANES, LANES), BF16),
            pltpu.VMEM((TAPS * LANES, LANES), BF16),
            pltpu.VMEM((8, LANES), F32),
            pltpu.VMEM((tiles, 8, LANES), F32),
            pltpu.VMEM((tiles, 8, LANES), F32),
            pltpu.VMEM((tiles, 8, LANES), F32),
            pltpu.VMEM((tiles, 8, LANES), F32),
            pltpu.VMEM((tiles, 8, LANES), F32),
            pltpu.VMEM((tiles, 8, LANES), F32),
            pltpu.SemaphoreType.DMA((2, 8)),
            pltpu.SemaphoreType.DMA((2, 8)),
            pltpu.SemaphoreType.DMA((2, 2 * stages)),
            pltpu.SemaphoreType.DMA((2, 2 * stages)),
        ],
        compiler_params=pltpu.CompilerParams(
            collective_id=0, has_side_effects=True, vmem_limit_bytes=48 * 1024 * 1024
        ),
    )(
        brick_slot.reshape(-1),
        fields,
        weight_one,
        weight_two,
        gain.reshape(1, channels),
        bias.reshape(1, channels),
    )

    def pack(values):
        return values[:, :, :4, :channels].astype(BF16).reshape(features.shape)

    return (
        pack(out),
        pack(grad_features),
        gw_one,
        gw_two,
        gg.reshape(channels),
        gb.reshape(channels),
    )


def solution(mesh):
    in_specs = (
        P("gx", "gy", None, None),
        P("gx", "gy", None, None),
        P("gx", "gy", None, None, None),
        P(),
        P(),
        P(),
        P(),
    )
    out_specs = (P("gx", "gy", None, None), P("gx", "gy", None, None), P(), P(), P(), P())
    return jax.shard_map(body, mesh=mesh, in_specs=in_specs, out_specs=out_specs, check_vma=False)
```

```python
import functools
import math

import jax
import jax.numpy as jnp
from jax import lax
from jax.experimental import pallas as pl
from jax.experimental.pallas import tpu as pltpu
from jax.sharding import PartitionSpec as P

F32 = jnp.float32
BF16 = jnp.bfloat16
MESH = pl.DeviceIdType.MESH
LANES = 128
TAPS = 27
OFFSETS = (-1, 0, 1)
DIRECTIONS = tuple((i, j) for i in OFFSETS for j in OFFSETS if (i, j) != (0, 0))


def source_range(step):
    return pl.ds(1, 8) if step == 0 else pl.ds(8 if step > 0 else 1, 1)


def landing_range(step):
    return pl.ds(1, 8) if step == 0 else pl.ds(0 if step > 0 else 9, 1)


RIDERS = (1, 4, 7, 10, 13, 16)
HOSTS = tuple(t for t in range(TAPS) if t not in RIDERS)
BLOCKS = len(HOSTS)


def rider(block):
    return (RIDERS[block // 3], block % 3) if block < 3 * len(RIDERS) else None


def sum_groups(size_x, size_y):
    groups = [("gx", 1, 2), ("gx", 2, size_x // 2), ("gy", 1, size_y)]
    return [group for group in groups if group[2] > 1]


def kernel(
    size_x, size_y, tiles, scale,
    slots, fields, w_one, w_two, gain_in, bias_in,
    out, grad_out, gw_one, gw_two, gg_out, gb_out,
    held, held_two, shifted, cols_a, cols_b, wm_one, wm_two, wt_one, wt_two, pad_rows,
    raw, w_here, red_a, red_b, in_a, in_b, all_a, all_b,
    halo_send, halo_recv, sum_send, sum_recv, all_send, all_recv, w_sem,
):
    px, py = lax.axis_index("gx"), lax.axis_index("gy")
    groups = sum_groups(size_x, size_y)
    stages = len(groups)
    loads = [
        pltpu.make_async_copy(w_in, w_here.at[n], w_sem.at[n])
        for n, w_in in enumerate((w_one, w_two))
    ]
    for load in loads:
        load.start()

    def exists(dx, dy):
        ok = None
        for pos, step, size in ((px, dx, size_x), (py, dy, size_y)):
            if step == 0:
                continue
            one = pos + step < size if step > 0 else pos >= 1
            ok = one if ok is None else jnp.logical_and(ok, one)
        return ok

    def at_step(dx, dy):
        return {"gx": px + dx, "gy": py + dy}

    def rank_in(group):
        axis, stride, count = group
        return lax.rem((px if axis == "gx" else py) // stride, count)

    def member(group, rank):
        axis, stride, _ = group
        move = (rank - rank_in(group)) * stride
        return at_step(move, 0) if axis == "gx" else at_step(0, move)

    held[...] = jnp.zeros_like(held)
    held_two[...] = jnp.zeros_like(held_two)

    barrier = pltpu.get_barrier_semaphore()
    greeted = jnp.int32(0)
    for dx, dy in DIRECTIONS:
        there = exists(dx, dy)
        greeted = greeted + jnp.where(there, 1, 0)

        @pl.when(there)
        def _(dx=dx, dy=dy):
            pl.semaphore_signal(barrier, inc=1, device_id=at_step(dx, dy), device_id_type=MESH)

    for group in groups:
        for turn in range(1, group[2]):
            other = lax.rem(rank_in(group) + turn, group[2])
            pl.semaphore_signal(
                barrier, inc=1, device_id=member(group, other), device_id_type=MESH
            )

    z_index = lax.broadcasted_iota(jnp.int32, (1, 8, LANES), 1)
    lane_index = lax.broadcasted_iota(jnp.int32, (1, 8, LANES), 2)
    low_half = jnp.where(z_index < 4, 1.0, 0.0).astype(F32)
    high_half = 1.0 - low_half
    cell_slot = [slots[0, 0, c // 4, c // 2 % 2, c % 2] for c in range(8)]

    def picks(i, j, s):
        cell = (i * 2 + j) * 2
        lower = jnp.where(cell_slot[cell] == s, 1.0, 0.0).astype(F32)
        upper = jnp.where(cell_slot[cell + 1] == s, 1.0, 0.0).astype(F32)
        return lower * low_half + upper * high_half

    masks = {(i, j, s): picks(i, j, s) for i in range(2) for j in range(2) for s in range(4)}
    filled = {
        (i, j): masks[i, j, 0] + masks[i, j, 1] + masks[i, j, 2] + masks[i, j, 3]
        for i in range(2)
        for j in range(2)
    }
    for f in range(2):
        for i in range(2):
            for j in range(2):
                total = fields[f, 0] * masks[i, j, 0]
                for s in range(1, 4):
                    total = total + fields[f, s] * masks[i, j, s]
                held[f, 1 + 4 * i : 5 + 4 * i, 1 + 4 * j : 5 + 4 * j] = total.reshape(
                    4, 4, 8, LANES
                )

    pl.semaphore_wait(barrier, greeted + sum(group[2] - 1 for group in groups))

    def halo_copy(buf, phase, number):
        dx, dy = DIRECTIONS[number]
        return pltpu.make_async_remote_copy(
            src_ref=buf.at[:, source_range(dx), source_range(dy)],
            dst_ref=buf.at[:, landing_range(dx), landing_range(dy)],
            send_sem=halo_send.at[phase, number],
            recv_sem=halo_recv.at[phase, number],
            device_id=at_step(dx, dy),
            device_id_type=MESH,
        )

    def halo_start(buf, phase):
        for number, (dx, dy) in enumerate(DIRECTIONS):

            @pl.when(exists(dx, dy))
            def _(number=number):
                halo_copy(buf, phase, number).start()

    def halo_arrive(buf, phase):
        for number, (dx, dy) in enumerate(DIRECTIONS):

            @pl.when(exists(-dx, -dy))
            def _(number=number):
                halo_copy(buf, phase, number).wait_recv()

    def halo_sent(buf, phase):
        for number, (dx, dy) in enumerate(DIRECTIONS):

            @pl.when(exists(dx, dy))
            def _(number=number):
                halo_copy(buf, phase, number).wait_send()

    halo_start(held, 0)

    raw[...] = jnp.zeros_like(raw)
    for n, (wide, turned) in enumerate(((wm_one, wt_one), (wm_two, wt_two))):
        loads[n].wait()
        for t in range(TAPS):
            raw[t * LANES : t * LANES + 96, 0:96] = w_here[n, t]
        turns = {}
        for t in range(TAPS):
            flip = (TAPS - 1 - t) * LANES
            turns[t] = raw[flip : flip + LANES, :].astype(F32).T.astype(BF16)
        for block, t in enumerate(HOSTS):
            at = block * LANES
            wide[at : at + LANES, :] = raw[t * LANES : (t + 1) * LANES, :]
            turned[at : at + LANES, :] = turns[t]
            if rider(block):
                extra, third = rider(block)
                rows = extra * LANES + third * 32
                wide[at + 96 : at + LANES, :] = raw[rows : rows + 32, :]
                turned[at + 96 : at + LANES, :] = turns[extra][third * 32 : third * 32 + 32]
    pad_rows[...] = jnp.zeros_like(pad_rows)
    pad_rows[0:1, 0:96] = gain_in[...]
    pad_rows[1:2, 0:96] = bias_in[...]
    gain = pad_rows[0:1, :]
    bias = pad_rows[1:2, :]
    red_a[...] = jnp.zeros_like(red_a)
    red_b[...] = jnp.zeros_like(red_b)

    def columns(buf, f, cols):
        values = buf[f].reshape(100, 8, LANES)
        shifted[1] = values.reshape(10, 10, 8, LANES)
        shifted[0] = jnp.where(z_index == 0, 0.0, pltpu.roll(values, 1, 1)).reshape(
            10, 10, 8, LANES
        )
        shifted[2] = jnp.where(z_index == 7, 0.0, pltpu.roll(values, 7, 1)).reshape(
            10, 10, 8, LANES
        )
        for third in range(3):
            turned = pltpu.roll(values, 96 - 32 * third, 2)
            shifted[3 + third] = jnp.where(lane_index >= 96, turned, 0.0).reshape(
                10, 10, 8, LANES
            )

        def window(t, version):
            a, b = t // 9, t // 3 % 3
            return shifted[version, a : a + 8, b : b + 8].reshape(512, LANES)

        for block, t in enumerate(HOSTS):
            values = window(t, t % 3)
            if rider(block):
                values = values + window(rider(block)[0], 3 + rider(block)[1])
            cols[:, block * LANES : (block + 1) * LANES] = values.astype(BF16)

    def dense_mask():
        rows = []
        for i in range(2):
            line = jnp.concatenate(
                [jnp.broadcast_to(filled[i, j], (4, 8, LANES)) for j in range(2)], axis=0
            )
            rows.append(jnp.broadcast_to(line[None], (4, 8, 8, LANES)))
        return jnp.concatenate(rows, axis=0).reshape(512, LANES)

    def interior(buf, f):
        return buf[f, 1:9, 1:9].reshape(512, LANES)

    def dot(lhs, rhs):
        return jnp.dot(lhs, rhs, preferred_element_type=F32)

    def weight_sums(left, cols, red):
        left_t = left.T.astype(BF16)[0:96]
        for block in range(BLOCKS):
            red[pl.ds(block * 12, 12)] = dot(
                left_t, cols[:, block * LANES : (block + 1) * LANES]
            ).reshape(12, 8, LANES)

    halo_arrive(held, 0)
    occupied = dense_mask()
    columns(held, 0, cols_a)
    first_conv = dot(cols_a[...], wm_one[...]) * occupied
    pre = first_conv * gain + bias
    sigmoid = 1.0 / (1.0 + jnp.exp(-pre))
    hidden = occupied * (pre * sigmoid)
    held_two[0, 1:9, 1:9] = hidden.reshape(8, 8, 8, LANES)
    columns(held, 1, cols_b)
    back_hidden = dot(cols_b[...], wt_two[...]) * occupied
    back_pre = back_hidden * (sigmoid * (1.0 + pre * (1.0 - sigmoid)))
    held_two[1, 1:9, 1:9] = (back_pre * gain).reshape(8, 8, 8, LANES)
    halo_start(held_two, 1)
    red_b[BLOCKS * 12, 0:1, :] = jnp.sum(back_pre * first_conv, axis=0, keepdims=True)
    red_b[BLOCKS * 12, 1:2, :] = jnp.sum(back_pre, axis=0, keepdims=True)

    reds, ins, alls = (red_a, red_b), (in_a, in_b), (all_a, all_b)
    offsets = ([jnp.int32(0)], [jnp.int32(0)])
    pieces, landings, first_sem = [], [], []
    length, landing, sems = tiles, 0, 0
    for group in groups:
        length = length // group[2]
        pieces.append(length)
        landings.append(landing)
        first_sem.append(sems)
        landing += length * (group[2] - 1)
        sems += group[2] - 1

    def scatter_copies(which, stage):
        group, piece = groups[stage], pieces[stage]
        copies = []
        for turn in range(1, group[2]):
            other = lax.rem(rank_in(group) + turn, group[2])
            sem = first_sem[stage] + turn - 1
            copies.append(
                pltpu.make_async_remote_copy(
                    src_ref=reds[which].at[pl.ds(offsets[which][stage] + other * piece, piece)],
                    dst_ref=ins[which].at[pl.ds(landings[stage] + (turn - 1) * piece, piece)],
                    send_sem=sum_send.at[which, sem],
                    recv_sem=sum_recv.at[which, sem],
                    device_id=member(group, other),
                    device_id_type=MESH,
                )
            )
        return copies

    def gather_copies(which, stage):
        group, piece = groups[stage], pieces[stage]
        copies = []
        for turn in range(1, group[2]):
            other = lax.rem(rank_in(group) + turn, group[2])
            sem = first_sem[stage] + turn - 1
            rows = alls[which].at[pl.ds(offsets[which][stage + 1] // 2, piece // 2)]
            copies.append(
                pltpu.make_async_remote_copy(
                    src_ref=rows,
                    dst_ref=rows,
                    send_sem=all_send.at[which, sem],
                    recv_sem=all_recv.at[which, sem],
                    device_id=member(group, other),
                    device_id_type=MESH,
                )
            )
        return copies

    def scatter_end(which, stage):
        group, piece = groups[stage], pieces[stage]
        for copy in scatter_copies(which, stage):
            copy.wait()
        keep = offsets[which][stage] + rank_in(group) * piece
        offsets[which].append(keep)
        total = reds[which][pl.ds(keep, piece)]
        for turn in range(group[2] - 1):
            total = total + ins[which][pl.ds(landings[stage] + turn * piece, piece)]
        if stage == stages - 1:
            alls[which][pl.ds(keep // 2, piece // 2)] = (
                (total * scale).reshape(piece // 2, 16, LANES).astype(BF16)
            )
        else:
            reds[which][pl.ds(keep, piece)] = total

    def advance(which, step):
        if step > 2 * stages:
            return
        if step > 0:
            if step <= stages:
                scatter_end(which, step - 1)
            else:
                for copy in gather_copies(which, 2 * stages - step):
                    copy.wait()
        if step < stages:
            copies = scatter_copies(which, step)
        elif step < 2 * stages:
            copies = gather_copies(which, 2 * stages - 1 - step)
        else:
            copies = []
        for copy in copies:
            copy.start()

    weight_sums(interior(held_two, 0), cols_b, red_a)
    advance(0, 0)
    halo_arrive(held_two, 1)
    columns(held_two, 1, cols_a)
    weight_sums(interior(held, 0), cols_a, red_b)
    advance(1, 0)
    advance(0, 1)

    def to_slots(dense, ref):
        dense = dense.reshape(8, 8, 8, LANES)
        for s in range(4):
            total = None
            for i in range(2):
                for j in range(2):
                    part = dense[4 * i : 4 * i + 4, 4 * j : 4 * j + 4].reshape(16, 8, LANES)
                    part = part * masks[i, j, s]
                    total = part if total is None else total + part
            ref[s] = (total + pltpu.roll(total, 4, 1))[:, 0:4, 0:96]

    to_slots(interior(held, 1) + dot(cols_a[...], wt_one[...]), grad_out)
    advance(1, 1)
    columns(held_two, 0, cols_b)
    advance(0, 2)
    to_slots(interior(held, 0) + dot(cols_b[...], wm_two[...]), out)
    def unpack(summed, gw):
        for block, t in enumerate(HOSTS):
            values = summed[pl.ds(block * 6, 6)].astype(F32).reshape(96, LANES)
            gw[TAPS - 1 - t] = values[:, 0:96]
            if rider(block):
                extra, third = rider(block)
                lanes = slice(third * 32, third * 32 + 32)
                gw[TAPS - 1 - extra, :, lanes] = pltpu.roll(values, third * 32 + 32, 1)[:, lanes]

    for step in range(2, 2 * stages + 1):
        advance(1, step)
        advance(0, step + 1)
        if step + 1 == 2 * stages:
            unpack(all_a, gw_two)
    unpack(all_b, gw_one)
    last = all_b[BLOCKS * 6].astype(F32)
    gg_out[...] = last[0:1, 0:96]
    gb_out[...] = last[1:2, 0:96]
    halo_sent(held, 0)
    halo_sent(held_two, 1)


def body(features, cotangent, brick_slot, weight_one, weight_two, gain, bias):
    count_slots = features.shape[2]
    channels = gain.shape[0]
    size_x, size_y = lax.axis_size("gx"), lax.axis_size("gy")
    devices = size_x * size_y
    scale = 1.0 / math.sqrt(devices * count_slots * 64)
    tiles = -(-(BLOCKS * 12 + 1) // (2 * devices)) * 2 * devices
    copies = sum(group[2] - 1 for group in sum_groups(size_x, size_y))
    fields = jnp.stack([features, cotangent]).reshape(2, count_slots, 16, 4, channels)
    fields = jnp.concatenate([fields, fields], axis=3).astype(F32)
    fields = jnp.pad(fields, ((0, 0), (0, 0), (0, 0), (0, 0), (0, LANES - channels)))
    vmem = pl.BlockSpec(memory_space=pltpu.VMEM)
    smem = pl.BlockSpec(memory_space=pltpu.SMEM)
    hbm = pl.BlockSpec(memory_space=pltpu.HBM)
    slot_shape = jax.ShapeDtypeStruct((count_slots, 16, 4, channels), F32)
    weight_shape = jax.ShapeDtypeStruct((TAPS, channels, channels), F32)
    row_shape = jax.ShapeDtypeStruct((1, channels), F32)
    out, grad_features, gw_one, gw_two, gg, gb = pl.pallas_call(
        functools.partial(kernel, size_x, size_y, tiles, scale),
        out_shape=(slot_shape, slot_shape, weight_shape, weight_shape, row_shape, row_shape),
        in_specs=[smem, vmem, hbm, hbm, vmem, vmem],
        out_specs=(vmem,) * 6,
        scratch_shapes=[
            pltpu.VMEM((2, 10, 10, 8, LANES), F32),
            pltpu.VMEM((2, 10, 10, 8, LANES), F32),
            pltpu.VMEM((6, 10, 10, 8, LANES), F32),
            pltpu.VMEM((512, BLOCKS * LANES), BF16),
            pltpu.VMEM((512, BLOCKS * LANES), BF16),
            pltpu.VMEM((BLOCKS * LANES, LANES), BF16),
            pltpu.VMEM((BLOCKS * LANES, LANES), BF16),
            pltpu.VMEM((BLOCKS * LANES, LANES), BF16),
            pltpu.VMEM((BLOCKS * LANES, LANES), BF16),
            pltpu.VMEM((8, LANES), F32),
            pltpu.VMEM((TAPS * LANES, LANES), BF16),
            pltpu.VMEM((2, TAPS, channels, channels), BF16),
            pltpu.VMEM((tiles, 8, LANES), F32),
            pltpu.VMEM((tiles, 8, LANES), F32),
            pltpu.VMEM((tiles, 8, LANES), F32),
            pltpu.VMEM((tiles, 8, LANES), F32),
            pltpu.VMEM((tiles // 2, 16, LANES), BF16),
            pltpu.VMEM((tiles // 2, 16, LANES), BF16),
            pltpu.SemaphoreType.DMA((2, 8)),
            pltpu.SemaphoreType.DMA((2, 8)),
            pltpu.SemaphoreType.DMA((2, copies)),
            pltpu.SemaphoreType.DMA((2, copies)),
            pltpu.SemaphoreType.DMA((2, copies)),
            pltpu.SemaphoreType.DMA((2, copies)),
            pltpu.SemaphoreType.DMA((2,)),
        ],
        compiler_params=pltpu.CompilerParams(
            collective_id=0, has_side_effects=True, vmem_limit_bytes=48 * 1024 * 1024
        ),
    )(
        brick_slot,
        fields,
        weight_one,
        weight_two,
        gain.reshape(1, channels),
        bias.reshape(1, channels),
    )

    def pack(values):
        return values.astype(BF16).reshape(features.shape)

    return (
        pack(out),
        pack(grad_features),
        gw_one,
        gw_two,
        gg.reshape(channels),
        gb.reshape(channels),
    )


def solution(mesh):
    in_specs = (
        P("gx", "gy", None, None),
        P("gx", "gy", None, None),
        P("gx", "gy", None, None, None),
        P(),
        P(),
        P(),
        P(),
    )
    out_specs = (P("gx", "gy", None, None), P("gx", "gy", None, None), P(), P(), P(), P())
    return jax.shard_map(body, mesh=mesh, in_specs=in_specs, out_specs=out_specs, check_vma=False)
```

```python
import functools
import math

import jax
import jax.numpy as jnp
from jax import lax
from jax.experimental import pallas as pl
from jax.experimental.pallas import tpu as pltpu
from jax.sharding import PartitionSpec as P

F32 = jnp.float32
BF16 = jnp.bfloat16
MESH = pl.DeviceIdType.MESH
LANES = 128
TAPS = 27
OFFSETS = (-1, 0, 1)
DIRECTIONS = tuple((i, j) for i in OFFSETS for j in OFFSETS if (i, j) != (0, 0))


def source_range(step):
    return pl.ds(1, 8) if step == 0 else pl.ds(8 if step > 0 else 1, 1)


def landing_range(step):
    return pl.ds(1, 8) if step == 0 else pl.ds(0 if step > 0 else 9, 1)


RIDERS = (1, 4, 7, 10, 13, 16)
HOSTS = tuple(t for t in range(TAPS) if t not in RIDERS)
BLOCKS = len(HOSTS)


def rider(block):
    return (RIDERS[block // 3], block % 3) if block < 3 * len(RIDERS) else None


def sum_groups(size_x, size_y):
    groups = [("gx", 1, 2), ("gx", 2, size_x // 2), ("gy", 1, size_y)]
    return [group for group in groups if group[2] > 1]


def kernel(
    size_x, size_y, tiles, scale,
    slots, fields, w_one, w_two, gain_in, bias_in,
    out, grad_out, gw_one, gw_two, gg_out, gb_out,
    held, held_two, shifted, cols_a, cols_b, wm_one, wm_two, wt_one, wt_two, pad_rows,
    raw, w_here, red_a, red_b, in_a, in_b, wire_a, wire_b, land_a, land_b, all_a, all_b,
    halo_send, halo_recv, sum_send, sum_recv, all_send, all_recv, w_sem,
):
    px, py = lax.axis_index("gx"), lax.axis_index("gy")
    groups = sum_groups(size_x, size_y)
    stages = len(groups)
    loads = [
        pltpu.make_async_copy(w_in, w_here.at[n], w_sem.at[n])
        for n, w_in in enumerate((w_one, w_two))
    ]
    for load in loads:
        load.start()

    def exists(dx, dy):
        ok = None
        for pos, step, size in ((px, dx, size_x), (py, dy, size_y)):
            if step == 0:
                continue
            one = pos + step < size if step > 0 else pos >= 1
            ok = one if ok is None else jnp.logical_and(ok, one)
        return ok

    def at_step(dx, dy):
        return {"gx": px + dx, "gy": py + dy}

    def rank_in(group):
        axis, stride, count = group
        return lax.rem((px if axis == "gx" else py) // stride, count)

    def member(group, rank):
        axis, stride, _ = group
        move = (rank - rank_in(group)) * stride
        return at_step(move, 0) if axis == "gx" else at_step(0, move)

    held[...] = jnp.zeros_like(held)
    held_two[...] = jnp.zeros_like(held_two)

    barrier = pltpu.get_barrier_semaphore()
    greeted = jnp.int32(0)
    for dx, dy in DIRECTIONS:
        there = exists(dx, dy)
        greeted = greeted + jnp.where(there, 1, 0)

        @pl.when(there)
        def _(dx=dx, dy=dy):
            pl.semaphore_signal(barrier, inc=1, device_id=at_step(dx, dy), device_id_type=MESH)

    for group in groups:
        for turn in range(1, group[2]):
            other = lax.rem(rank_in(group) + turn, group[2])
            pl.semaphore_signal(
                barrier, inc=1, device_id=member(group, other), device_id_type=MESH
            )

    z_index = lax.broadcasted_iota(jnp.int32, (1, 8, LANES), 1)
    lane_index = lax.broadcasted_iota(jnp.int32, (1, 8, LANES), 2)
    low_half = jnp.where(z_index < 4, 1.0, 0.0).astype(F32)
    high_half = 1.0 - low_half
    cell_slot = [slots[0, 0, c // 4, c // 2 % 2, c % 2] for c in range(8)]

    def picks(i, j, s):
        cell = (i * 2 + j) * 2
        lower = jnp.where(cell_slot[cell] == s, 1.0, 0.0).astype(F32)
        upper = jnp.where(cell_slot[cell + 1] == s, 1.0, 0.0).astype(F32)
        return lower * low_half + upper * high_half

    masks = {(i, j, s): picks(i, j, s) for i in range(2) for j in range(2) for s in range(4)}
    filled = {
        (i, j): masks[i, j, 0] + masks[i, j, 1] + masks[i, j, 2] + masks[i, j, 3]
        for i in range(2)
        for j in range(2)
    }
    for f in range(2):
        for i in range(2):
            for j in range(2):
                total = fields[f, 0] * masks[i, j, 0]
                for s in range(1, 4):
                    total = total + fields[f, s] * masks[i, j, s]
                held[f, 1 + 4 * i : 5 + 4 * i, 1 + 4 * j : 5 + 4 * j] = total.reshape(
                    4, 4, 8, LANES
                )

    pl.semaphore_wait(barrier, greeted + sum(group[2] - 1 for group in groups))

    def halo_copy(buf, phase, number):
        dx, dy = DIRECTIONS[number]
        return pltpu.make_async_remote_copy(
            src_ref=buf.at[:, source_range(dx), source_range(dy)],
            dst_ref=buf.at[:, landing_range(dx), landing_range(dy)],
            send_sem=halo_send.at[phase, number],
            recv_sem=halo_recv.at[phase, number],
            device_id=at_step(dx, dy),
            device_id_type=MESH,
        )

    def halo_start(buf, phase):
        for number, (dx, dy) in enumerate(DIRECTIONS):

            @pl.when(exists(dx, dy))
            def _(number=number):
                halo_copy(buf, phase, number).start()

    def halo_arrive(buf, phase):
        for number, (dx, dy) in enumerate(DIRECTIONS):

            @pl.when(exists(-dx, -dy))
            def _(number=number):
                halo_copy(buf, phase, number).wait_recv()

    def halo_sent(buf, phase):
        for number, (dx, dy) in enumerate(DIRECTIONS):

            @pl.when(exists(dx, dy))
            def _(number=number):
                halo_copy(buf, phase, number).wait_send()

    halo_start(held, 0)

    raw[...] = jnp.zeros_like(raw)

    def load_raw(n):
        loads[n].wait()
        for t in range(TAPS):
            raw[n, t * LANES : t * LANES + 96, 0:96] = w_here[n, t]

    def widen(n, wide):
        for block, t in enumerate(HOSTS):
            at = block * LANES
            wide[at : at + LANES, :] = raw[n, t * LANES : (t + 1) * LANES, :]
            if rider(block):
                extra, third = rider(block)
                rows = extra * LANES + third * 32
                wide[at + 96 : at + LANES, :] = raw[n, rows : rows + 32, :]

    def flip(n, turned):
        turns = {}
        for t in range(TAPS):
            rows = (TAPS - 1 - t) * LANES
            turns[t] = raw[n, rows : rows + LANES, :].astype(F32).T.astype(BF16)
        for block, t in enumerate(HOSTS):
            at = block * LANES
            turned[at : at + LANES, :] = turns[t]
            if rider(block):
                extra, third = rider(block)
                turned[at + 96 : at + LANES, :] = turns[extra][third * 32 : third * 32 + 32]

    load_raw(0)
    widen(0, wm_one)
    load_raw(1)
    flip(1, wt_two)
    pad_rows[...] = jnp.zeros_like(pad_rows)
    pad_rows[0:1, 0:96] = gain_in[...]
    pad_rows[1:2, 0:96] = bias_in[...]
    gain = pad_rows[0:1, :]
    bias = pad_rows[1:2, :]
    red_a[...] = jnp.zeros_like(red_a)
    red_b[...] = jnp.zeros_like(red_b)

    def columns(buf, f, cols):
        values = buf[f].reshape(100, 8, LANES)
        shifted[1] = values.reshape(10, 10, 8, LANES)
        shifted[0] = jnp.where(z_index == 0, 0.0, pltpu.roll(values, 1, 1)).reshape(
            10, 10, 8, LANES
        )
        shifted[2] = jnp.where(z_index == 7, 0.0, pltpu.roll(values, 7, 1)).reshape(
            10, 10, 8, LANES
        )
        for third in range(3):
            turned = pltpu.roll(values, 96 - 32 * third, 2)
            shifted[3 + third] = jnp.where(lane_index >= 96, turned, 0.0).reshape(
                10, 10, 8, LANES
            )

        def window(t, version):
            a, b = t // 9, t // 3 % 3
            return shifted[version, a : a + 8, b : b + 8].reshape(512, LANES)

        for block, t in enumerate(HOSTS):
            values = window(t, t % 3)
            if rider(block):
                values = values + window(rider(block)[0], 3 + rider(block)[1])
            cols[:, block * LANES : (block + 1) * LANES] = values.astype(BF16)

    def dense_mask():
        rows = []
        for i in range(2):
            line = jnp.concatenate(
                [jnp.broadcast_to(filled[i, j], (4, 8, LANES)) for j in range(2)], axis=0
            )
            rows.append(jnp.broadcast_to(line[None], (4, 8, 8, LANES)))
        return jnp.concatenate(rows, axis=0).reshape(512, LANES)

    def interior(buf, f):
        return buf[f, 1:9, 1:9].reshape(512, LANES)

    def dot(lhs, rhs):
        return jnp.dot(lhs, rhs, preferred_element_type=F32)

    def weight_sums(left, cols, red):
        left_t = left.T.astype(BF16)[0:96]
        for block in range(BLOCKS):
            red[pl.ds(block * 12, 12)] = dot(
                left_t, cols[:, block * LANES : (block + 1) * LANES]
            ).reshape(12, 8, LANES)

    halo_arrive(held, 0)
    occupied = dense_mask()
    columns(held, 0, cols_a)
    first_conv = dot(cols_a[...], wm_one[...]) * occupied
    pre = first_conv * gain + bias
    sigmoid = 1.0 / (1.0 + jnp.exp(-pre))
    hidden = occupied * (pre * sigmoid)
    held_two[0, 1:9, 1:9] = hidden.reshape(8, 8, 8, LANES)
    columns(held, 1, cols_b)
    back_hidden = dot(cols_b[...], wt_two[...]) * occupied
    back_pre = back_hidden * (sigmoid * (1.0 + pre * (1.0 - sigmoid)))
    held_two[1, 1:9, 1:9] = (back_pre * gain).reshape(8, 8, 8, LANES)
    halo_start(held_two, 1)
    red_b[BLOCKS * 12, 0:1, :] = jnp.sum(back_pre * first_conv, axis=0, keepdims=True)
    red_b[BLOCKS * 12, 1:2, :] = jnp.sum(back_pre, axis=0, keepdims=True)

    reds, ins, alls = (red_a, red_b), (in_a, in_b), (all_a, all_b)
    wires, lands = (wire_a, wire_b), (land_a, land_b)
    offsets = ([jnp.int32(0)], [jnp.int32(0)])
    pieces, landings, first_sem = [], [], []
    length, landing, sems = tiles, 0, 0
    narrow = [stage > 0 and group[1] > 1 for stage, group in enumerate(groups)]
    for group in groups:
        length = length // group[2]
        pieces.append(length)
        landings.append(landing)
        first_sem.append(sems)
        landing += length * (group[2] - 1)
        sems += group[2] - 1

    def scatter_copies(which, stage):
        group, piece = groups[stage], pieces[stage]
        copies = []
        for turn in range(1, group[2]):
            other = lax.rem(rank_in(group) + turn, group[2])
            sem = first_sem[stage] + turn - 1
            if narrow[stage]:
                half = piece // 2
                source = wires[which].at[pl.ds(other * half, half)]
                target = lands[which].at[pl.ds((turn - 1) * half, half)]
            else:
                source = reds[which].at[pl.ds(offsets[which][stage] + other * piece, piece)]
                target = ins[which].at[pl.ds(landings[stage] + (turn - 1) * piece, piece)]
            copies.append(
                pltpu.make_async_remote_copy(
                    src_ref=source,
                    dst_ref=target,
                    send_sem=sum_send.at[which, sem],
                    recv_sem=sum_recv.at[which, sem],
                    device_id=member(group, other),
                    device_id_type=MESH,
                )
            )
        return copies

    def gather_copies(which, stage):
        group, piece = groups[stage], pieces[stage]
        copies = []
        for turn in range(1, group[2]):
            other = lax.rem(rank_in(group) + turn, group[2])
            sem = first_sem[stage] + turn - 1
            rows = alls[which].at[pl.ds(offsets[which][stage + 1] // 2, piece // 2)]
            copies.append(
                pltpu.make_async_remote_copy(
                    src_ref=rows,
                    dst_ref=rows,
                    send_sem=all_send.at[which, sem],
                    recv_sem=all_recv.at[which, sem],
                    device_id=member(group, other),
                    device_id_type=MESH,
                )
            )
        return copies

    def scatter_end(which, stage):
        group, piece = groups[stage], pieces[stage]
        for copy in scatter_copies(which, stage):
            copy.wait()
        keep = offsets[which][stage] + rank_in(group) * piece
        offsets[which].append(keep)
        total = reds[which][pl.ds(keep, piece)]
        for turn in range(group[2] - 1):
            if narrow[stage]:
                half = piece // 2
                came = lands[which][pl.ds(turn * half, half)].astype(F32)
                total = total + came.reshape(piece, 8, LANES)
            else:
                total = total + ins[which][pl.ds(landings[stage] + turn * piece, piece)]
        if stage < stages - 1:
            reds[which][pl.ds(keep, piece)] = total
            if narrow[stage + 1]:
                wires[which][...] = total.reshape(piece // 2, 16, LANES).astype(BF16)
            return
        total = total * scale
        if which == 1:
            rest = total - total.astype(BF16).astype(F32)
            tile = lax.broadcasted_iota(jnp.int32, total.shape, 0) + keep
            row = lax.broadcasted_iota(jnp.int32, total.shape, 1)
            mine = jnp.logical_and(tile == BLOCKS * 12, jnp.logical_and(row >= 2, row < 4))
            total = jnp.where(mine, pltpu.roll(rest, 2, 1), total)
        alls[which][pl.ds(keep // 2, piece // 2)] = total.reshape(
            piece // 2, 16, LANES
        ).astype(BF16)

    def advance(which, step):
        if step > 2 * stages:
            return
        if step > 0:
            if step <= stages:
                scatter_end(which, step - 1)
            else:
                for copy in gather_copies(which, 2 * stages - step):
                    copy.wait()
        if step < stages:
            copies = scatter_copies(which, step)
        elif step < 2 * stages:
            copies = gather_copies(which, 2 * stages - 1 - step)
        else:
            copies = []
        for copy in copies:
            copy.start()

    weight_sums(interior(held_two, 1), cols_a, red_b)
    advance(1, 0)
    weight_sums(interior(held_two, 0), cols_b, red_a)
    advance(0, 0)
    flip(0, wt_one)
    advance(1, 1)
    halo_arrive(held_two, 1)
    columns(held_two, 1, cols_a)
    advance(0, 1)

    def to_slots(dense, ref):
        dense = dense.reshape(8, 8, 8, LANES)
        for s in range(4):
            total = None
            for i in range(2):
                for j in range(2):
                    part = dense[4 * i : 4 * i + 4, 4 * j : 4 * j + 4].reshape(16, 8, LANES)
                    part = part * masks[i, j, s]
                    total = part if total is None else total + part
            ref[s] = (total + pltpu.roll(total, 4, 1))[:, 0:4, 0:96]

    to_slots(interior(held, 1) + dot(cols_a[...], wt_one[...]), grad_out)
    advance(1, 2)
    widen(1, wm_two)
    columns(held_two, 0, cols_b)
    advance(1, 3)
    advance(0, 2)
    to_slots(interior(held, 0) + dot(cols_b[...], wm_two[...]), out)
    advance(1, 4)
    advance(0, 3)
    for step in range(5, 2 * stages + 1):
        advance(1, step)
        advance(0, step - 1)
    for block, t in enumerate(HOSTS):
        values = all_b[pl.ds(block * 6, 6)].astype(F32).reshape(96, LANES).T
        gw_one[t] = values[0:96, :]
        if rider(block):
            extra, third = rider(block)
            gw_one[extra, third * 32 : third * 32 + 32, :] = values[96:LANES, :]
    last = all_b[BLOCKS * 6].astype(F32)
    last = last + pltpu.roll(last, 14, 0)
    advance(0, 2 * stages)
    for block, t in enumerate(HOSTS):
        values = all_a[pl.ds(block * 6, 6)].astype(F32).reshape(96, LANES)
        gw_two[TAPS - 1 - t] = values[:, 0:96]
        if rider(block):
            extra, third = rider(block)
            lanes = slice(third * 32, third * 32 + 32)
            gw_two[TAPS - 1 - extra, :, lanes] = pltpu.roll(values, third * 32 + 32, 1)[:, lanes]
    gg_out[...] = last[0:1, 0:96]
    gb_out[...] = last[1:2, 0:96]
    halo_sent(held, 0)
    halo_sent(held_two, 1)


def body(features, cotangent, brick_slot, weight_one, weight_two, gain, bias):
    count_slots = features.shape[2]
    channels = gain.shape[0]
    size_x, size_y = lax.axis_size("gx"), lax.axis_size("gy")
    devices = size_x * size_y
    scale = 1.0 / math.sqrt(devices * count_slots * 64)
    tiles = -(-(BLOCKS * 12 + 1) // (2 * devices)) * 2 * devices
    copies = sum(group[2] - 1 for group in sum_groups(size_x, size_y))
    fields = jnp.stack([features, cotangent]).reshape(2, count_slots, 16, 4, channels)
    fields = jnp.concatenate([fields, fields], axis=3).astype(F32)
    fields = jnp.pad(fields, ((0, 0), (0, 0), (0, 0), (0, 0), (0, LANES - channels)))
    vmem = pl.BlockSpec(memory_space=pltpu.VMEM)
    smem = pl.BlockSpec(memory_space=pltpu.SMEM)
    hbm = pl.BlockSpec(memory_space=pltpu.HBM)
    slot_shape = jax.ShapeDtypeStruct((count_slots, 16, 4, channels), F32)
    weight_shape = jax.ShapeDtypeStruct((TAPS, channels, channels), F32)
    row_shape = jax.ShapeDtypeStruct((1, channels), F32)
    out, grad_features, gw_one, gw_two, gg, gb = pl.pallas_call(
        functools.partial(kernel, size_x, size_y, tiles, scale),
        out_shape=(slot_shape, slot_shape, weight_shape, weight_shape, row_shape, row_shape),
        in_specs=[smem, vmem, hbm, hbm, vmem, vmem],
        out_specs=(vmem,) * 6,
        scratch_shapes=[
            pltpu.VMEM((2, 10, 10, 8, LANES), F32),
            pltpu.VMEM((2, 10, 10, 8, LANES), F32),
            pltpu.VMEM((6, 10, 10, 8, LANES), F32),
            pltpu.VMEM((512, BLOCKS * LANES), BF16),
            pltpu.VMEM((512, BLOCKS * LANES), BF16),
            pltpu.VMEM((BLOCKS * LANES, LANES), BF16),
            pltpu.VMEM((BLOCKS * LANES, LANES), BF16),
            pltpu.VMEM((BLOCKS * LANES, LANES), BF16),
            pltpu.VMEM((BLOCKS * LANES, LANES), BF16),
            pltpu.VMEM((8, LANES), F32),
            pltpu.VMEM((2, TAPS * LANES, LANES), BF16),
            pltpu.VMEM((2, TAPS, channels, channels), BF16),
            pltpu.VMEM((tiles, 8, LANES), F32),
            pltpu.VMEM((tiles, 8, LANES), F32),
            pltpu.VMEM((tiles, 8, LANES), F32),
            pltpu.VMEM((tiles, 8, LANES), F32),
            pltpu.VMEM((tiles // 4, 16, LANES), BF16),
            pltpu.VMEM((tiles // 4, 16, LANES), BF16),
            pltpu.VMEM((tiles // 4, 16, LANES), BF16),
            pltpu.VMEM((tiles // 4, 16, LANES), BF16),
            pltpu.VMEM((tiles // 2, 16, LANES), BF16),
            pltpu.VMEM((tiles // 2, 16, LANES), BF16),
            pltpu.SemaphoreType.DMA((2, 8)),
            pltpu.SemaphoreType.DMA((2, 8)),
            pltpu.SemaphoreType.DMA((2, copies)),
            pltpu.SemaphoreType.DMA((2, copies)),
            pltpu.SemaphoreType.DMA((2, copies)),
            pltpu.SemaphoreType.DMA((2, copies)),
            pltpu.SemaphoreType.DMA((2,)),
        ],
        compiler_params=pltpu.CompilerParams(
            collective_id=0, has_side_effects=True, vmem_limit_bytes=62 * 1024 * 1024
        ),
    )(
        brick_slot,
        fields,
        weight_one,
        weight_two,
        gain.reshape(1, channels),
        bias.reshape(1, channels),
    )

    def pack(values):
        return values.astype(BF16).reshape(features.shape)

    return (
        pack(out),
        pack(grad_features),
        gw_one,
        gw_two,
        gg.reshape(channels),
        gb.reshape(channels),
    )


def solution(mesh):
    in_specs = (
        P("gx", "gy", None, None),
        P("gx", "gy", None, None),
        P("gx", "gy", None, None, None),
        P(),
        P(),
        P(),
        P(),
    )
    out_specs = (P("gx", "gy", None, None), P("gx", "gy", None, None), P(), P(), P(), P())
    return jax.shard_map(body, mesh=mesh, in_specs=in_specs, out_specs=out_specs, check_vma=False)
```

```python
import functools
import math

import jax
import jax.numpy as jnp
from jax import lax
from jax.experimental import pallas as pl
from jax.experimental.pallas import tpu as pltpu
from jax.sharding import PartitionSpec as P

F32 = jnp.float32
BF16 = jnp.bfloat16
MESH = pl.DeviceIdType.MESH
LANES = 128
TAPS = 27
OFFSETS = (-1, 0, 1)
DIRECTIONS = tuple((i, j) for i in OFFSETS for j in OFFSETS if (i, j) != (0, 0))


def source_range(step):
    return pl.ds(1, 8) if step == 0 else pl.ds(8 if step > 0 else 1, 1)


def landing_range(step):
    return pl.ds(1, 8) if step == 0 else pl.ds(0 if step > 0 else 9, 1)


PLANE_RIDERS = (1, 4)
PLANE_HOSTS = (0, 2, 3, 5, 6, 7, 8)
PLANE = len(PLANE_HOSTS)
HOSTS = tuple(9 * a + u for a in range(3) for u in PLANE_HOSTS)
BLOCKS = len(HOSTS)


def rider(block):
    a, n = divmod(block, PLANE)
    return (9 * a + PLANE_RIDERS[n // 3], n % 3) if n < 6 else None


def sum_groups(size_x, size_y):
    groups = [("gx", 1, 2), ("gx", 2, size_x // 2), ("gy", 1, size_y)]
    return [group for group in groups if group[2] > 1]


def kernel(
    size_x, size_y, tiles, scale,
    small, fields, w_one, w_two,
    out, grad_out, gw_one, gw_two, gg_out, gb_out,
    held, held_two, shifted, cols_a, cols_b, wm_one, wm_two, wt_one, wt_two,
    raw, w_here, red_a, red_b, in_a, in_b, wire_a, wire_b, land_a, land_b, all_a, all_b,
    halo_send, halo_recv, sum_send, sum_recv, all_send, all_recv, w_sem,
):
    px, py = lax.axis_index("gx"), lax.axis_index("gy")
    groups = sum_groups(size_x, size_y)
    stages = len(groups)
    loads = [
        pltpu.make_async_copy(w_in, w_here.at[n], w_sem.at[n])
        for n, w_in in enumerate((w_one, w_two))
    ]
    for load in loads:
        load.start()

    def exists(dx, dy):
        ok = None
        for pos, step, size in ((px, dx, size_x), (py, dy, size_y)):
            if step == 0:
                continue
            one = pos + step < size if step > 0 else pos >= 1
            ok = one if ok is None else jnp.logical_and(ok, one)
        return ok

    def at_step(dx, dy):
        return {"gx": px + dx, "gy": py + dy}

    def rank_in(group):
        axis, stride, count = group
        return lax.rem((px if axis == "gx" else py) // stride, count)

    def member(group, rank):
        axis, stride, _ = group
        move = (rank - rank_in(group)) * stride
        return at_step(move, 0) if axis == "gx" else at_step(0, move)

    held[...] = jnp.zeros_like(held)
    held_two[...] = jnp.zeros_like(held_two)

    barrier = pltpu.get_barrier_semaphore()
    greeted = jnp.int32(0)
    for dx, dy in DIRECTIONS:
        there = exists(dx, dy)
        greeted = greeted + jnp.where(there, 1, 0)

        @pl.when(there)
        def _(dx=dx, dy=dy):
            pl.semaphore_signal(barrier, inc=1, device_id=at_step(dx, dy), device_id_type=MESH)

    for group in groups:
        for turn in range(1, group[2]):
            other = lax.rem(rank_in(group) + turn, group[2])
            pl.semaphore_signal(
                barrier, inc=1, device_id=member(group, other), device_id_type=MESH
            )

    z_index = lax.broadcasted_iota(jnp.int32, (1, 8, LANES), 1)
    lane_index = lax.broadcasted_iota(jnp.int32, (1, 8, LANES), 2)
    low_half = jnp.where(z_index < 4, 1.0, 0.0).astype(F32)
    high_half = 1.0 - low_half
    cell_slot = [small[8 + c : 9 + c, :].reshape(1, 1, LANES) for c in range(8)]

    def picks(i, j, s):
        cell = (i * 2 + j) * 2
        lower = 1.0 - jnp.minimum(jnp.abs(cell_slot[cell] - s), 1.0)
        upper = 1.0 - jnp.minimum(jnp.abs(cell_slot[cell + 1] - s), 1.0)
        return lower * low_half + upper * high_half

    masks = {(i, j, s): picks(i, j, s) for i in range(2) for j in range(2) for s in range(4)}
    filled = {
        (i, j): masks[i, j, 0] + masks[i, j, 1] + masks[i, j, 2] + masks[i, j, 3]
        for i in range(2)
        for j in range(2)
    }
    for f in range(2):
        for i in range(2):
            for j in range(2):
                total = fields[f, 0] * masks[i, j, 0]
                for s in range(1, 4):
                    total = total + fields[f, s] * masks[i, j, s]
                held[f, 1 + 4 * i : 5 + 4 * i, 1 + 4 * j : 5 + 4 * j] = total.reshape(
                    4, 4, 8, LANES
                )

    pl.semaphore_wait(barrier, greeted + sum(group[2] - 1 for group in groups))

    def halo_copy(buf, phase, number):
        dx, dy = DIRECTIONS[number]
        return pltpu.make_async_remote_copy(
            src_ref=buf.at[:, source_range(dx), source_range(dy)],
            dst_ref=buf.at[:, landing_range(dx), landing_range(dy)],
            send_sem=halo_send.at[phase, number],
            recv_sem=halo_recv.at[phase, number],
            device_id=at_step(dx, dy),
            device_id_type=MESH,
        )

    def halo_start(buf, phase):
        for number, (dx, dy) in enumerate(DIRECTIONS):

            @pl.when(exists(dx, dy))
            def _(number=number):
                halo_copy(buf, phase, number).start()

    def halo_arrive(buf, phase):
        for number, (dx, dy) in enumerate(DIRECTIONS):

            @pl.when(exists(-dx, -dy))
            def _(number=number):
                halo_copy(buf, phase, number).wait_recv()

    def halo_sent(buf, phase):
        for number, (dx, dy) in enumerate(DIRECTIONS):

            @pl.when(exists(dx, dy))
            def _(number=number):
                halo_copy(buf, phase, number).wait_send()

    halo_start(held, 0)

    raw[...] = jnp.zeros_like(raw)

    def load_raw(n):
        loads[n].wait()
        for t in range(TAPS):
            raw[n, t * LANES : t * LANES + 96, 0:96] = w_here[n, t]

    def widen(n, wide):
        for block, t in enumerate(HOSTS):
            at = block * LANES
            wide[at : at + LANES, :] = raw[n, t * LANES : (t + 1) * LANES, :]
            if rider(block):
                extra, third = rider(block)
                rows = extra * LANES + third * 32
                wide[at + 96 : at + LANES, :] = raw[n, rows : rows + 32, :]

    def flip(n, turned):
        turns = {}
        for t in range(TAPS):
            rows = (TAPS - 1 - t) * LANES
            turns[t] = raw[n, rows : rows + LANES, :].astype(F32).T.astype(BF16)
        for block, t in enumerate(HOSTS):
            at = block * LANES
            turned[at : at + LANES, :] = turns[t]
            if rider(block):
                extra, third = rider(block)
                turned[at + 96 : at + LANES, :] = turns[extra][third * 32 : third * 32 + 32]

    load_raw(0)
    widen(0, wm_one)
    load_raw(1)
    flip(1, wt_two)
    gain = small[0:1, :]
    bias = small[1:2, :]
    red_a[...] = jnp.zeros_like(red_a)
    red_b[...] = jnp.zeros_like(red_b)

    def columns(buf, f, cols):
        values = buf[f].reshape(100, 8, LANES)
        shifted[1] = values.reshape(10, 10, 8, LANES)
        shifted[0] = jnp.where(z_index == 0, 0.0, pltpu.roll(values, 1, 1)).reshape(
            10, 10, 8, LANES
        )
        shifted[2] = jnp.where(z_index == 7, 0.0, pltpu.roll(values, 7, 1)).reshape(
            10, 10, 8, LANES
        )
        for third in range(3):
            turned = pltpu.roll(values, 96 - 32 * third, 2)
            shifted[3 + third] = jnp.where(lane_index >= 96, turned, 0.0).reshape(
                10, 10, 8, LANES
            )

        def window(u, version):
            b = u // 3 % 3
            return shifted[version, :, b : b + 8].reshape(640, LANES)

        for block, u in enumerate(PLANE_HOSTS):
            values = window(u, u % 3)
            if rider(block):
                values = values + window(rider(block)[0], 3 + rider(block)[1])
            cols[:, block * LANES : (block + 1) * LANES] = values.astype(BF16)

    def dense_mask():
        rows = []
        for i in range(2):
            line = jnp.concatenate(
                [jnp.broadcast_to(filled[i, j], (4, 8, LANES)) for j in range(2)], axis=0
            )
            rows.append(jnp.broadcast_to(line[None], (4, 8, 8, LANES)))
        return jnp.concatenate(rows, axis=0).reshape(512, LANES)

    def interior(buf, f):
        return buf[f, 1:9, 1:9].reshape(512, LANES)

    def dot(lhs, rhs):
        return jnp.dot(lhs, rhs, preferred_element_type=F32)

    def conv(cols, wide):
        total = None
        for a in range(3):
            part = dot(
                cols[64 * a : 64 * a + 512, :],
                wide[a * PLANE * LANES : (a + 1) * PLANE * LANES, :],
            )
            total = part if total is None else total + part
        return total

    def weight_sums(left, cols, red):
        left_t = left.T.astype(BF16)[0:96]
        for a in range(3):
            for n in range(0, PLANE, 2):
                last = min(n + 2, PLANE)
                product = dot(left_t, cols[64 * a : 64 * a + 512, n * LANES : last * LANES])
                for k in range(last - n):
                    red[pl.ds((a * PLANE + n + k) * 12, 12)] = product[
                        :, k * LANES : (k + 1) * LANES
                    ].reshape(12, 8, LANES)

    halo_arrive(held, 0)
    occupied = dense_mask()
    columns(held, 0, cols_a)
    first_conv = conv(cols_a, wm_one) * occupied
    pre = first_conv * gain + bias
    sigmoid = 1.0 / (1.0 + jnp.exp(-pre))
    hidden = occupied * (pre * sigmoid)
    held_two[0, 1:9, 1:9] = hidden.reshape(8, 8, 8, LANES)
    columns(held, 1, cols_b)
    back_hidden = conv(cols_b, wt_two) * occupied
    back_pre = back_hidden * (sigmoid * (1.0 + pre * (1.0 - sigmoid)))
    held_two[1, 1:9, 1:9] = (back_pre * gain).reshape(8, 8, 8, LANES)
    halo_start(held_two, 1)
    red_b[BLOCKS * 12, 0:1, :] = jnp.sum(back_pre * first_conv, axis=0, keepdims=True)
    red_b[BLOCKS * 12, 1:2, :] = jnp.sum(back_pre, axis=0, keepdims=True)

    reds, ins, alls = (red_a, red_b), (in_a, in_b), (all_a, all_b)
    wires, lands = (wire_a, wire_b), (land_a, land_b)
    offsets = ([jnp.int32(0)], [jnp.int32(0)])
    pieces, landings, first_sem = [], [], []
    length, landing, sems = tiles, 0, 0
    narrow = [stage > 0 and group[1] > 1 for stage, group in enumerate(groups)]
    for group in groups:
        length = length // group[2]
        pieces.append(length)
        landings.append(landing)
        first_sem.append(sems)
        landing += length * (group[2] - 1)
        sems += group[2] - 1

    def scatter_copies(which, stage):
        group, piece = groups[stage], pieces[stage]
        copies = []
        for turn in range(1, group[2]):
            other = lax.rem(rank_in(group) + turn, group[2])
            sem = first_sem[stage] + turn - 1
            if narrow[stage]:
                half = piece // 2
                source = wires[which].at[pl.ds(other * half, half)]
                target = lands[which].at[pl.ds((turn - 1) * half, half)]
            else:
                source = reds[which].at[pl.ds(offsets[which][stage] + other * piece, piece)]
                target = ins[which].at[pl.ds(landings[stage] + (turn - 1) * piece, piece)]
            copies.append(
                pltpu.make_async_remote_copy(
                    src_ref=source,
                    dst_ref=target,
                    send_sem=sum_send.at[which, sem],
                    recv_sem=sum_recv.at[which, sem],
                    device_id=member(group, other),
                    device_id_type=MESH,
                )
            )
        return copies

    def gather_copies(which, stage):
        group, piece = groups[stage], pieces[stage]
        copies = []
        for turn in range(1, group[2]):
            other = lax.rem(rank_in(group) + turn, group[2])
            sem = first_sem[stage] + turn - 1
            rows = alls[which].at[pl.ds(offsets[which][stage + 1] // 2, piece // 2)]
            copies.append(
                pltpu.make_async_remote_copy(
                    src_ref=rows,
                    dst_ref=rows,
                    send_sem=all_send.at[which, sem],
                    recv_sem=all_recv.at[which, sem],
                    device_id=member(group, other),
                    device_id_type=MESH,
                )
            )
        return copies

    def scatter_end(which, stage):
        group, piece = groups[stage], pieces[stage]
        for copy in scatter_copies(which, stage):
            copy.wait()
        keep = offsets[which][stage] + rank_in(group) * piece
        offsets[which].append(keep)
        total = reds[which][pl.ds(keep, piece)]
        for turn in range(group[2] - 1):
            if narrow[stage]:
                half = piece // 2
                came = lands[which][pl.ds(turn * half, half)].astype(F32)
                total = total + came.reshape(piece, 8, LANES)
            else:
                total = total + ins[which][pl.ds(landings[stage] + turn * piece, piece)]
        if stage < stages - 1:
            reds[which][pl.ds(keep, piece)] = total
            if narrow[stage + 1]:
                wires[which][...] = total.reshape(piece // 2, 16, LANES).astype(BF16)
            return
        total = total * scale
        if which == 1:
            rest = total - total.astype(BF16).astype(F32)
            tile = lax.broadcasted_iota(jnp.int32, total.shape, 0) + keep
            row = lax.broadcasted_iota(jnp.int32, total.shape, 1)
            mine = jnp.logical_and(tile == BLOCKS * 12, jnp.logical_and(row >= 2, row < 4))
            total = jnp.where(mine, pltpu.roll(rest, 2, 1), total)
        alls[which][pl.ds(keep // 2, piece // 2)] = total.reshape(
            piece // 2, 16, LANES
        ).astype(BF16)

    def advance(which, step):
        if step > 2 * stages:
            return
        if step > 0:
            if step <= stages:
                scatter_end(which, step - 1)
            else:
                for copy in gather_copies(which, 2 * stages - step):
                    copy.wait()
        if step < stages:
            copies = scatter_copies(which, step)
        elif step < 2 * stages:
            copies = gather_copies(which, 2 * stages - 1 - step)
        else:
            copies = []
        for copy in copies:
            copy.start()

    weight_sums(interior(held_two, 1), cols_a, red_b)
    advance(1, 0)
    weight_sums(interior(held_two, 0), cols_b, red_a)
    advance(0, 0)
    flip(0, wt_one)
    advance(1, 1)
    halo_arrive(held_two, 1)
    columns(held_two, 1, cols_a)
    advance(0, 1)

    def to_slots(dense, ref):
        dense = dense.reshape(8, 8, 8, LANES)
        for s in range(4):
            total = None
            for i in range(2):
                for j in range(2):
                    part = dense[4 * i : 4 * i + 4, 4 * j : 4 * j + 4].reshape(16, 8, LANES)
                    part = part * masks[i, j, s]
                    total = part if total is None else total + part
            ref[s] = (total + pltpu.roll(total, 4, 1))[:, 0:4, 0:96]

    back_inputs = conv(cols_a, wt_one)
    advance(1, 2)
    to_slots(interior(held, 1) + back_inputs, grad_out)
    advance(0, 2)
    widen(1, wm_two)
    columns(held_two, 0, cols_b)
    advance(1, 3)
    second_conv = conv(cols_b, wm_two)
    advance(0, 3)
    advance(1, 4)
    to_slots(interior(held, 0) + second_conv, out)
    for step in range(5, 2 * stages + 1):
        advance(1, step)
        advance(0, step - 1)
    for block, t in enumerate(HOSTS):
        values = all_b[pl.ds(block * 6, 6)].astype(F32).reshape(96, LANES).T
        gw_one[t] = values[0:96, :]
        if rider(block):
            extra, third = rider(block)
            gw_one[extra, third * 32 : third * 32 + 32, :] = values[96:LANES, :]
    last = all_b[BLOCKS * 6].astype(F32)
    last = last + pltpu.roll(last, 14, 0)
    advance(0, 2 * stages)
    for block, t in enumerate(HOSTS):
        values = all_a[pl.ds(block * 6, 6)].astype(F32).reshape(96, LANES)
        gw_two[TAPS - 1 - t] = values[:, 0:96]
        if rider(block):
            extra, third = rider(block)
            lanes = slice(third * 32, third * 32 + 32)
            gw_two[TAPS - 1 - extra, :, lanes] = pltpu.roll(values, third * 32 + 32, 1)[:, lanes]
    gg_out[...] = last[0:1, 0:96]
    gb_out[...] = last[1:2, 0:96]
    halo_sent(held, 0)
    halo_sent(held_two, 1)


def body(features, cotangent, brick_slot, weight_one, weight_two, gain, bias):
    count_slots = features.shape[2]
    channels = gain.shape[0]
    size_x, size_y = lax.axis_size("gx"), lax.axis_size("gy")
    devices = size_x * size_y
    scale = 1.0 / math.sqrt(devices * count_slots * 64)
    tiles = -(-(BLOCKS * 12 + 1) // (2 * devices)) * 2 * devices
    copies = sum(group[2] - 1 for group in sum_groups(size_x, size_y))
    fields = jnp.stack([features, cotangent]).reshape(2, count_slots, 16, 4, channels)
    fields = jnp.concatenate([fields, fields], axis=3).astype(F32)
    fields = jnp.pad(fields, ((0, 0), (0, 0), (0, 0), (0, 0), (0, LANES - channels)))
    spare = ((0, 0), (0, LANES - channels))
    small = jnp.concatenate(
        [
            jnp.pad(gain.reshape(1, channels), spare),
            jnp.pad(bias.reshape(1, channels), spare),
            jnp.zeros((6, LANES), F32),
            jnp.broadcast_to(brick_slot.reshape(8, 1).astype(F32), (8, LANES)),
        ]
    )
    vmem = pl.BlockSpec(memory_space=pltpu.VMEM)
    hbm = pl.BlockSpec(memory_space=pltpu.HBM)
    slot_shape = jax.ShapeDtypeStruct((count_slots, 16, 4, channels), F32)
    weight_shape = jax.ShapeDtypeStruct((TAPS, channels, channels), F32)
    row_shape = jax.ShapeDtypeStruct((1, channels), F32)
    out, grad_features, gw_one, gw_two, gg, gb = pl.pallas_call(
        functools.partial(kernel, size_x, size_y, tiles, scale),
        out_shape=(slot_shape, slot_shape, weight_shape, weight_shape, row_shape, row_shape),
        in_specs=[vmem, vmem, hbm, hbm],
        out_specs=(vmem,) * 6,
        scratch_shapes=[
            pltpu.VMEM((2, 10, 10, 8, LANES), F32),
            pltpu.VMEM((2, 10, 10, 8, LANES), F32),
            pltpu.VMEM((6, 10, 10, 8, LANES), F32),
            pltpu.VMEM((640, PLANE * LANES), BF16),
            pltpu.VMEM((640, PLANE * LANES), BF16),
            pltpu.VMEM((BLOCKS * LANES, LANES), BF16),
            pltpu.VMEM((BLOCKS * LANES, LANES), BF16),
            pltpu.VMEM((BLOCKS * LANES, LANES), BF16),
            pltpu.VMEM((BLOCKS * LANES, LANES), BF16),
            pltpu.VMEM((2, TAPS * LANES, LANES), BF16),
            pltpu.VMEM((2, TAPS, channels, channels), BF16),
            pltpu.VMEM((tiles, 8, LANES), F32),
            pltpu.VMEM((tiles, 8, LANES), F32),
            pltpu.VMEM((tiles, 8, LANES), F32),
            pltpu.VMEM((tiles, 8, LANES), F32),
            pltpu.VMEM((tiles // 4, 16, LANES), BF16),
            pltpu.VMEM((tiles // 4, 16, LANES), BF16),
            pltpu.VMEM((tiles // 4, 16, LANES), BF16),
            pltpu.VMEM((tiles // 4, 16, LANES), BF16),
            pltpu.VMEM((tiles // 2, 16, LANES), BF16),
            pltpu.VMEM((tiles // 2, 16, LANES), BF16),
            pltpu.SemaphoreType.DMA((2, 8)),
            pltpu.SemaphoreType.DMA((2, 8)),
            pltpu.SemaphoreType.DMA((2, copies)),
            pltpu.SemaphoreType.DMA((2, copies)),
            pltpu.SemaphoreType.DMA((2, copies)),
            pltpu.SemaphoreType.DMA((2, copies)),
            pltpu.SemaphoreType.DMA((2,)),
        ],
        compiler_params=pltpu.CompilerParams(
            collective_id=0, has_side_effects=True, vmem_limit_bytes=48 * 1024 * 1024
        ),
    )(
        small,
        fields,
        weight_one,
        weight_two,
    )

    def pack(values):
        return values.astype(BF16).reshape(features.shape)

    return (
        pack(out),
        pack(grad_features),
        gw_one,
        gw_two,
        gg.reshape(channels),
        gb.reshape(channels),
    )


def solution(mesh):
    in_specs = (
        P("gx", "gy", None, None),
        P("gx", "gy", None, None),
        P("gx", "gy", None, None, None),
        P(),
        P(),
        P(),
        P(),
    )
    out_specs = (P("gx", "gy", None, None), P("gx", "gy", None, None), P(), P(), P(), P())
    return jax.shard_map(body, mesh=mesh, in_specs=in_specs, out_specs=out_specs, check_vma=False)
```

```python
import functools
import math

import jax
import jax.numpy as jnp
from jax import lax
from jax.experimental import pallas as pl
from jax.experimental.pallas import tpu as pltpu
from jax.sharding import PartitionSpec as P

F32 = jnp.float32
BF16 = jnp.bfloat16
MESH = pl.DeviceIdType.MESH
LANES = 128
TAPS = 27
OFFSETS = (-1, 0, 1)
DIRECTIONS = tuple((i, j) for i in OFFSETS for j in OFFSETS if (i, j) != (0, 0))


def source_range(step):
    return pl.ds(1, 8) if step == 0 else pl.ds(8 if step > 0 else 1, 1)


def landing_range(step):
    return pl.ds(1, 8) if step == 0 else pl.ds(0 if step > 0 else 9, 1)


PLANE_RIDERS = (1, 4)
PLANE_HOSTS = (0, 2, 3, 5, 6, 7, 8)
PLANE = len(PLANE_HOSTS)
HOSTS = tuple(9 * a + u for a in range(3) for u in PLANE_HOSTS)
BLOCKS = len(HOSTS)


def rider(block):
    a, n = divmod(block, PLANE)
    return (9 * a + PLANE_RIDERS[n // 3], n % 3) if n < 6 else None


def sum_groups(size_x, size_y):
    groups = [("gx", 1, 2), ("gx", 2, size_x // 2), ("gy", 1, size_y)]
    return [group for group in groups if group[2] > 1]


def kernel(
    size_x, size_y, tiles, scale,
    small, fields, w_one, w_two,
    out, grad_out, gw_one, gw_two, gg_out, gb_out,
    held, held_two, shifted, cols_a, cols_b, wm_one, wm_two, wt_one, wt_two,
    raw, w_here, red_a, red_b, in_a, in_b, wire_a, wire_b, land_a, land_b, all_a, all_b,
    halo_send, halo_recv, sum_send, sum_recv, all_send, all_recv, w_sem,
):
    px, py = lax.axis_index("gx"), lax.axis_index("gy")
    groups = sum_groups(size_x, size_y)
    stages = len(groups)
    loads = [
        pltpu.make_async_copy(w_in, w_here.at[n], w_sem.at[n])
        for n, w_in in enumerate((w_one, w_two))
    ]
    for load in loads:
        load.start()

    def exists(dx, dy):
        ok = None
        for pos, step, size in ((px, dx, size_x), (py, dy, size_y)):
            if step == 0:
                continue
            one = pos + step < size if step > 0 else pos >= 1
            ok = one if ok is None else jnp.logical_and(ok, one)
        return ok

    def at_step(dx, dy):
        return {"gx": px + dx, "gy": py + dy}

    def rank_in(group):
        axis, stride, count = group
        return lax.rem((px if axis == "gx" else py) // stride, count)

    def member(group, rank):
        axis, stride, _ = group
        move = (rank - rank_in(group)) * stride
        return at_step(move, 0) if axis == "gx" else at_step(0, move)

    held[...] = jnp.zeros_like(held)
    held_two[...] = jnp.zeros_like(held_two)

    barrier = pltpu.get_barrier_semaphore()
    greeted = jnp.int32(0)
    for dx, dy in DIRECTIONS:
        there = exists(dx, dy)
        greeted = greeted + jnp.where(there, 1, 0)

        @pl.when(there)
        def _(dx=dx, dy=dy):
            pl.semaphore_signal(barrier, inc=1, device_id=at_step(dx, dy), device_id_type=MESH)

    for group in groups:
        for turn in range(1, group[2]):
            other = lax.rem(rank_in(group) + turn, group[2])
            pl.semaphore_signal(
                barrier, inc=1, device_id=member(group, other), device_id_type=MESH
            )

    z_index = lax.broadcasted_iota(jnp.int32, (1, 8, LANES), 1)
    lane_index = lax.broadcasted_iota(jnp.int32, (1, 8, LANES), 2)
    low_half = jnp.where(z_index < 4, 1.0, 0.0).astype(F32)
    high_half = 1.0 - low_half
    cell_slot = [small[8 + c : 9 + c, :].reshape(1, 1, LANES) for c in range(8)]

    def picks(i, j, s):
        cell = (i * 2 + j) * 2
        lower = 1.0 - jnp.minimum(jnp.abs(cell_slot[cell] - s), 1.0)
        upper = 1.0 - jnp.minimum(jnp.abs(cell_slot[cell + 1] - s), 1.0)
        return lower * low_half + upper * high_half

    masks = {(i, j, s): picks(i, j, s) for i in range(2) for j in range(2) for s in range(4)}
    filled = {
        (i, j): masks[i, j, 0] + masks[i, j, 1] + masks[i, j, 2] + masks[i, j, 3]
        for i in range(2)
        for j in range(2)
    }
    for f in range(2):
        for i in range(2):
            for j in range(2):
                total = fields[f, 0] * masks[i, j, 0]
                for s in range(1, 4):
                    total = total + fields[f, s] * masks[i, j, s]
                held[f, 1 + 4 * i : 5 + 4 * i, 1 + 4 * j : 5 + 4 * j] = total.reshape(
                    4, 4, 8, LANES
                )

    pl.semaphore_wait(barrier, greeted + sum(group[2] - 1 for group in groups))

    def halo_copy(buf, phase, number):
        dx, dy = DIRECTIONS[number]
        return pltpu.make_async_remote_copy(
            src_ref=buf.at[:, source_range(dx), source_range(dy)],
            dst_ref=buf.at[:, landing_range(dx), landing_range(dy)],
            send_sem=halo_send.at[phase, number],
            recv_sem=halo_recv.at[phase, number],
            device_id=at_step(dx, dy),
            device_id_type=MESH,
        )

    def halo_start(buf, phase):
        for number, (dx, dy) in enumerate(DIRECTIONS):

            @pl.when(exists(dx, dy))
            def _(number=number):
                halo_copy(buf, phase, number).start()

    def halo_arrive(buf, phase):
        for number, (dx, dy) in enumerate(DIRECTIONS):

            @pl.when(exists(-dx, -dy))
            def _(number=number):
                halo_copy(buf, phase, number).wait_recv()

    def halo_sent(buf, phase):
        for number, (dx, dy) in enumerate(DIRECTIONS):

            @pl.when(exists(dx, dy))
            def _(number=number):
                halo_copy(buf, phase, number).wait_send()

    halo_start(held, 0)

    raw[...] = jnp.zeros_like(raw)

    def load_raw(n):
        loads[n].wait()
        for t in range(TAPS):
            raw[n, t * LANES : t * LANES + 96, 0:96] = w_here[n, t]

    def widen(n, wide):
        for block, t in enumerate(HOSTS):
            at = block * LANES
            wide[at : at + LANES, :] = raw[n, t * LANES : (t + 1) * LANES, :]
            if rider(block):
                extra, third = rider(block)
                rows = extra * LANES + third * 32
                wide[at + 96 : at + LANES, :] = raw[n, rows : rows + 32, :]

    def flip(n, turned):
        turns = {}
        for t in range(TAPS):
            rows = (TAPS - 1 - t) * LANES
            turns[t] = raw[n, rows : rows + LANES, :].astype(F32).T.astype(BF16)
        for block, t in enumerate(HOSTS):
            at = block * LANES
            turned[at : at + LANES, :] = turns[t]
            if rider(block):
                extra, third = rider(block)
                turned[at + 96 : at + LANES, :] = turns[extra][third * 32 : third * 32 + 32]

    load_raw(0)
    widen(0, wm_one)
    load_raw(1)
    flip(1, wt_two)
    gain = small[0:1, :]
    bias = small[1:2, :]
    red_a[...] = jnp.zeros_like(red_a)
    red_b[...] = jnp.zeros_like(red_b)

    def columns(buf, f, cols):
        values = buf[f].reshape(100, 8, LANES)
        shifted[1] = values.reshape(10, 10, 8, LANES)
        shifted[0] = jnp.where(z_index == 0, 0.0, pltpu.roll(values, 1, 1)).reshape(
            10, 10, 8, LANES
        )
        shifted[2] = jnp.where(z_index == 7, 0.0, pltpu.roll(values, 7, 1)).reshape(
            10, 10, 8, LANES
        )
        for third in range(3):
            turned = pltpu.roll(values, 96 - 32 * third, 2)
            shifted[3 + third] = jnp.where(lane_index >= 96, turned, 0.0).reshape(
                10, 10, 8, LANES
            )

        def window(u, version):
            b = u // 3 % 3
            return shifted[version, :, b : b + 8].reshape(640, LANES)

        for block, u in enumerate(PLANE_HOSTS):
            values = window(u, u % 3)
            if rider(block):
                values = values + window(rider(block)[0], 3 + rider(block)[1])
            cols[:, block * LANES : (block + 1) * LANES] = values.astype(BF16)

    def dense_mask():
        rows = []
        for i in range(2):
            line = jnp.concatenate(
                [jnp.broadcast_to(filled[i, j], (4, 8, LANES)) for j in range(2)], axis=0
            )
            rows.append(jnp.broadcast_to(line[None], (4, 8, 8, LANES)))
        return jnp.concatenate(rows, axis=0).reshape(512, LANES)

    def interior(buf, f):
        return buf[f, 1:9, 1:9].reshape(512, LANES)

    def dot(lhs, rhs):
        return jnp.dot(lhs, rhs, preferred_element_type=F32)

    def conv(cols, wide):
        total = None
        for a in range(3):
            part = dot(
                cols[64 * a : 64 * a + 512, :],
                wide[a * PLANE * LANES : (a + 1) * PLANE * LANES, :],
            )
            total = part if total is None else total + part
        return total

    def weight_sums(left, cols, red):
        left_t = left.T.astype(BF16)[0:96]
        for a in range(3):
            for n in range(0, PLANE, 2):
                last = min(n + 2, PLANE)
                product = dot(left_t, cols[64 * a : 64 * a + 512, n * LANES : last * LANES])
                for k in range(last - n):
                    red[pl.ds((a * PLANE + n + k) * 12, 12)] = product[
                        :, k * LANES : (k + 1) * LANES
                    ].reshape(12, 8, LANES)

    reds, ins, alls = (red_a, red_b), (in_a, in_b), (all_a, all_b)
    wires, lands = (wire_a, wire_b), (land_a, land_b)
    offsets = ([jnp.int32(0)], [jnp.int32(0)])
    pieces, landings, first_sem = [], [], []
    length, landing, sems = tiles, 0, 0
    narrow = [stage > 0 and group[1] > 1 for stage, group in enumerate(groups)]
    for group in groups:
        length = length // group[2]
        pieces.append(length)
        landings.append(landing)
        first_sem.append(sems)
        landing += length * (group[2] - 1)
        sems += group[2] - 1

    def scatter_copies(which, stage):
        group, piece = groups[stage], pieces[stage]
        copies = []
        for turn in range(1, group[2]):
            other = lax.rem(rank_in(group) + turn, group[2])
            sem = first_sem[stage] + turn - 1
            if narrow[stage]:
                half = piece // 2
                source = wires[which].at[pl.ds(other * half, half)]
                target = lands[which].at[pl.ds((turn - 1) * half, half)]
            else:
                source = reds[which].at[pl.ds(offsets[which][stage] + other * piece, piece)]
                target = ins[which].at[pl.ds(landings[stage] + (turn - 1) * piece, piece)]
            copies.append(
                pltpu.make_async_remote_copy(
                    src_ref=source,
                    dst_ref=target,
                    send_sem=sum_send.at[which, sem],
                    recv_sem=sum_recv.at[which, sem],
                    device_id=member(group, other),
                    device_id_type=MESH,
                )
            )
        return copies

    def gather_copies(which, stage):
        group, piece = groups[stage], pieces[stage]
        copies = []
        for turn in range(1, group[2]):
            other = lax.rem(rank_in(group) + turn, group[2])
            sem = first_sem[stage] + turn - 1
            rows = alls[which].at[pl.ds(offsets[which][stage + 1] // 2, piece // 2)]
            copies.append(
                pltpu.make_async_remote_copy(
                    src_ref=rows,
                    dst_ref=rows,
                    send_sem=all_send.at[which, sem],
                    recv_sem=all_recv.at[which, sem],
                    device_id=member(group, other),
                    device_id_type=MESH,
                )
            )
        return copies

    def scatter_end(which, stage):
        group, piece = groups[stage], pieces[stage]
        for copy in scatter_copies(which, stage):
            copy.wait()
        keep = offsets[which][stage] + rank_in(group) * piece
        offsets[which].append(keep)
        total = reds[which][pl.ds(keep, piece)]
        for turn in range(group[2] - 1):
            if narrow[stage]:
                half = piece // 2
                came = lands[which][pl.ds(turn * half, half)].astype(F32)
                total = total + came.reshape(piece, 8, LANES)
            else:
                total = total + ins[which][pl.ds(landings[stage] + turn * piece, piece)]
        if stage < stages - 1:
            reds[which][pl.ds(keep, piece)] = total
            if narrow[stage + 1]:
                wires[which][...] = total.reshape(piece // 2, 16, LANES).astype(BF16)
            return
        total = total * scale
        if which == 1:
            rest = total - total.astype(BF16).astype(F32)
            tile = lax.broadcasted_iota(jnp.int32, total.shape, 0) + keep
            row = lax.broadcasted_iota(jnp.int32, total.shape, 1)
            mine = jnp.logical_and(tile == BLOCKS * 12, jnp.logical_and(row >= 2, row < 4))
            total = jnp.where(mine, pltpu.roll(rest, 2, 1), total)
        alls[which][pl.ds(keep // 2, piece // 2)] = total.reshape(
            piece // 2, 16, LANES
        ).astype(BF16)

    def advance(which, step):
        if step > 2 * stages:
            return
        if step > 0:
            if step <= stages:
                scatter_end(which, step - 1)
            else:
                for copy in gather_copies(which, 2 * stages - step):
                    copy.wait()
        if step < stages:
            copies = scatter_copies(which, step)
        elif step < 2 * stages:
            copies = gather_copies(which, 2 * stages - 1 - step)
        else:
            copies = []
        for copy in copies:
            copy.start()

    halo_arrive(held, 0)
    occupied = dense_mask()
    columns(held, 0, cols_a)
    first_conv = conv(cols_a, wm_one) * occupied
    pre = first_conv * gain + bias
    sigmoid = 1.0 / (1.0 + jnp.exp(-pre))
    hidden = occupied * (pre * sigmoid)
    held_two[0, 1:9, 1:9] = hidden.reshape(8, 8, 8, LANES)
    columns(held, 1, cols_b)
    weight_sums(hidden, cols_b, red_a)
    advance(0, 0)
    back_hidden = conv(cols_b, wt_two) * occupied
    back_pre = back_hidden * (sigmoid * (1.0 + pre * (1.0 - sigmoid)))
    held_two[1, 1:9, 1:9] = (back_pre * gain).reshape(8, 8, 8, LANES)
    halo_start(held_two, 1)
    red_b[BLOCKS * 12, 0:1, :] = jnp.sum(back_pre * first_conv, axis=0, keepdims=True)
    red_b[BLOCKS * 12, 1:2, :] = jnp.sum(back_pre, axis=0, keepdims=True)

    advance(0, 1)
    weight_sums(interior(held_two, 1), cols_a, red_b)
    advance(1, 0)
    flip(0, wt_one)
    advance(1, 1)
    advance(0, 2)
    halo_arrive(held_two, 1)
    columns(held_two, 1, cols_a)

    def to_slots(dense, ref):
        dense = dense.reshape(8, 8, 8, LANES)
        for s in range(4):
            total = None
            for i in range(2):
                for j in range(2):
                    part = dense[4 * i : 4 * i + 4, 4 * j : 4 * j + 4].reshape(16, 8, LANES)
                    part = part * masks[i, j, s]
                    total = part if total is None else total + part
            ref[s] = (total + pltpu.roll(total, 4, 1))[:, 0:4, 0:96]

    to_slots(interior(held, 1) + conv(cols_a, wt_one), grad_out)
    widen(1, wm_two)
    columns(held_two, 0, cols_b)
    advance(1, 2)
    second_conv = conv(cols_b, wm_two)
    advance(0, 3)
    to_slots(interior(held, 0) + second_conv, out)
    advance(0, 4)
    advance(1, 3)
    advance(1, 4)
    for step in range(5, 2 * stages + 1):
        advance(0, step)
    for block, t in enumerate(HOSTS):
        values = all_a[pl.ds(block * 6, 6)].astype(F32).reshape(96, LANES)
        gw_two[TAPS - 1 - t] = values[:, 0:96]
        if rider(block):
            extra, third = rider(block)
            lanes = slice(third * 32, third * 32 + 32)
            gw_two[TAPS - 1 - extra, :, lanes] = pltpu.roll(values, third * 32 + 32, 1)[:, lanes]
    for step in range(5, 2 * stages + 1):
        advance(1, step)
    for block, t in enumerate(HOSTS):
        values = all_b[pl.ds(block * 6, 6)].astype(F32).reshape(96, LANES).T
        gw_one[t] = values[0:96, :]
        if rider(block):
            extra, third = rider(block)
            gw_one[extra, third * 32 : third * 32 + 32, :] = values[96:LANES, :]
    last = all_b[BLOCKS * 6].astype(F32)
    last = last + pltpu.roll(last, 14, 0)
    gg_out[...] = last[0:1, 0:96]
    gb_out[...] = last[1:2, 0:96]
    halo_sent(held, 0)
    halo_sent(held_two, 1)


def body(features, cotangent, brick_slot, weight_one, weight_two, gain, bias):
    count_slots = features.shape[2]
    channels = gain.shape[0]
    size_x, size_y = lax.axis_size("gx"), lax.axis_size("gy")
    devices = size_x * size_y
    scale = 1.0 / math.sqrt(devices * count_slots * 64)
    tiles = -(-(BLOCKS * 12 + 1) // (2 * devices)) * 2 * devices
    copies = sum(group[2] - 1 for group in sum_groups(size_x, size_y))
    fields = jnp.stack([features, cotangent]).reshape(2, count_slots, 16, 4, channels)
    fields = jnp.concatenate([fields, fields], axis=3).astype(F32)
    fields = jnp.pad(fields, ((0, 0), (0, 0), (0, 0), (0, 0), (0, LANES - channels)))
    spare = ((0, 0), (0, LANES - channels))
    small = jnp.concatenate(
        [
            jnp.pad(gain.reshape(1, channels), spare),
            jnp.pad(bias.reshape(1, channels), spare),
            jnp.zeros((6, LANES), F32),
            jnp.broadcast_to(brick_slot.reshape(8, 1).astype(F32), (8, LANES)),
        ]
    )
    vmem = pl.BlockSpec(memory_space=pltpu.VMEM)
    hbm = pl.BlockSpec(memory_space=pltpu.HBM)
    slot_shape = jax.ShapeDtypeStruct((count_slots, 16, 4, channels), F32)
    weight_shape = jax.ShapeDtypeStruct((TAPS, channels, channels), F32)
    row_shape = jax.ShapeDtypeStruct((1, channels), F32)
    out, grad_features, gw_one, gw_two, gg, gb = pl.pallas_call(
        functools.partial(kernel, size_x, size_y, tiles, scale),
        out_shape=(slot_shape, slot_shape, weight_shape, weight_shape, row_shape, row_shape),
        in_specs=[vmem, vmem, hbm, hbm],
        out_specs=(vmem,) * 6,
        scratch_shapes=[
            pltpu.VMEM((2, 10, 10, 8, LANES), F32),
            pltpu.VMEM((2, 10, 10, 8, LANES), F32),
            pltpu.VMEM((6, 10, 10, 8, LANES), F32),
            pltpu.VMEM((640, PLANE * LANES), BF16),
            pltpu.VMEM((640, PLANE * LANES), BF16),
            pltpu.VMEM((BLOCKS * LANES, LANES), BF16),
            pltpu.VMEM((BLOCKS * LANES, LANES), BF16),
            pltpu.VMEM((BLOCKS * LANES, LANES), BF16),
            pltpu.VMEM((BLOCKS * LANES, LANES), BF16),
            pltpu.VMEM((2, TAPS * LANES, LANES), BF16),
            pltpu.VMEM((2, TAPS, channels, channels), BF16),
            pltpu.VMEM((tiles, 8, LANES), F32),
            pltpu.VMEM((tiles, 8, LANES), F32),
            pltpu.VMEM((tiles, 8, LANES), F32),
            pltpu.VMEM((tiles, 8, LANES), F32),
            pltpu.VMEM((tiles // 4, 16, LANES), BF16),
            pltpu.VMEM((tiles // 4, 16, LANES), BF16),
            pltpu.VMEM((tiles // 4, 16, LANES), BF16),
            pltpu.VMEM((tiles // 4, 16, LANES), BF16),
            pltpu.VMEM((tiles // 2, 16, LANES), BF16),
            pltpu.VMEM((tiles // 2, 16, LANES), BF16),
            pltpu.SemaphoreType.DMA((2, 8)),
            pltpu.SemaphoreType.DMA((2, 8)),
            pltpu.SemaphoreType.DMA((2, copies)),
            pltpu.SemaphoreType.DMA((2, copies)),
            pltpu.SemaphoreType.DMA((2, copies)),
            pltpu.SemaphoreType.DMA((2, copies)),
            pltpu.SemaphoreType.DMA((2,)),
        ],
        compiler_params=pltpu.CompilerParams(
            collective_id=0, has_side_effects=True, vmem_limit_bytes=48 * 1024 * 1024
        ),
    )(
        small,
        fields,
        weight_one,
        weight_two,
    )

    def pack(values):
        return values.astype(BF16).reshape(features.shape)

    return (
        pack(out),
        pack(grad_features),
        gw_one,
        gw_two,
        gg.reshape(channels),
        gb.reshape(channels),
    )


def solution(mesh):
    in_specs = (
        P("gx", "gy", None, None),
        P("gx", "gy", None, None),
        P("gx", "gy", None, None, None),
        P(),
        P(),
        P(),
        P(),
    )
    out_specs = (P("gx", "gy", None, None), P("gx", "gy", None, None), P(), P(), P(), P())
    return jax.shard_map(body, mesh=mesh, in_specs=in_specs, out_specs=out_specs, check_vma=False)
```

```python
import functools
import math

import jax
import jax.numpy as jnp
from jax import lax
from jax.experimental import pallas as pl
from jax.experimental.pallas import tpu as pltpu
from jax.sharding import PartitionSpec as P

F32 = jnp.float32
BF16 = jnp.bfloat16
MESH = pl.DeviceIdType.MESH
LANES = 128
TAPS = 27
OFFSETS = (-1, 0, 1)
DIRECTIONS = tuple((i, j) for i in OFFSETS for j in OFFSETS if (i, j) != (0, 0))


def source_range(step):
    return pl.ds(1, 8) if step == 0 else pl.ds(8 if step > 0 else 1, 1)


def landing_range(step):
    return pl.ds(1, 8) if step == 0 else pl.ds(0 if step > 0 else 9, 1)


PLANE_RIDERS = (1, 4)
PLANE_HOSTS = (0, 2, 3, 5, 6, 7, 8)
PLANE = len(PLANE_HOSTS)
HOSTS = tuple(9 * a + u for a in range(3) for u in PLANE_HOSTS)
BLOCKS = len(HOSTS)


def rider(block):
    a, n = divmod(block, PLANE)
    return (9 * a + PLANE_RIDERS[n // 3], n % 3) if n < 6 else None


def sum_groups(size_x, size_y):
    groups = [("gx", 1, 2), ("gx", 2, size_x // 2), ("gy", 1, size_y)]
    return [group for group in groups if group[2] > 1]


def kernel(
    size_x, size_y, tiles, scale,
    small, fields, w_one, w_two,
    out, grad_out, gw_one, gw_two, gg_out, gb_out,
    held, held_two, shifted, cols_a, cols_b, wm_one, wm_two, wt_one, wt_two,
    raw, w_here, red_a, red_b, in_a, in_b, wire_a, wire_b, land_a, land_b, all_a, all_b,
    halo_send, halo_recv, sum_send, sum_recv, all_send, all_recv, w_sem,
):
    px, py = lax.axis_index("gx"), lax.axis_index("gy")
    groups = sum_groups(size_x, size_y)
    stages = len(groups)
    loads = [
        pltpu.make_async_copy(w_in, w_here.at[n], w_sem.at[n])
        for n, w_in in enumerate((w_one, w_two))
    ]
    for load in loads:
        load.start()

    def exists(dx, dy):
        ok = None
        for pos, step, size in ((px, dx, size_x), (py, dy, size_y)):
            if step == 0:
                continue
            one = pos + step < size if step > 0 else pos >= 1
            ok = one if ok is None else jnp.logical_and(ok, one)
        return ok

    def at_step(dx, dy):
        return {"gx": px + dx, "gy": py + dy}

    def rank_in(group):
        axis, stride, count = group
        return lax.rem((px if axis == "gx" else py) // stride, count)

    def member(group, rank):
        axis, stride, _ = group
        move = (rank - rank_in(group)) * stride
        return at_step(move, 0) if axis == "gx" else at_step(0, move)

    held[...] = jnp.zeros_like(held)
    held_two[...] = jnp.zeros_like(held_two)

    barrier = pltpu.get_barrier_semaphore()
    greeted = jnp.int32(0)
    for dx, dy in DIRECTIONS:
        there = exists(dx, dy)
        greeted = greeted + jnp.where(there, 1, 0)

        @pl.when(there)
        def _(dx=dx, dy=dy):
            pl.semaphore_signal(barrier, inc=1, device_id=at_step(dx, dy), device_id_type=MESH)

    for group in groups:
        for turn in range(1, group[2]):
            other = lax.rem(rank_in(group) + turn, group[2])
            pl.semaphore_signal(
                barrier, inc=1, device_id=member(group, other), device_id_type=MESH
            )

    z_index = lax.broadcasted_iota(jnp.int32, (1, 8, LANES), 1)
    lane_index = lax.broadcasted_iota(jnp.int32, (1, 8, LANES), 2)
    low_half = jnp.where(z_index < 4, 1.0, 0.0).astype(F32)
    high_half = 1.0 - low_half
    cell_slot = [small[8 + c : 9 + c, :].reshape(1, 1, LANES) for c in range(8)]

    def picks(i, j, s):
        cell = (i * 2 + j) * 2
        lower = 1.0 - jnp.minimum(jnp.abs(cell_slot[cell] - s), 1.0)
        upper = 1.0 - jnp.minimum(jnp.abs(cell_slot[cell + 1] - s), 1.0)
        return lower * low_half + upper * high_half

    masks = {(i, j, s): picks(i, j, s) for i in range(2) for j in range(2) for s in range(4)}
    filled = {
        (i, j): masks[i, j, 0] + masks[i, j, 1] + masks[i, j, 2] + masks[i, j, 3]
        for i in range(2)
        for j in range(2)
    }
    for f in range(2):
        for i in range(2):
            for j in range(2):
                total = fields[f, 0] * masks[i, j, 0]
                for s in range(1, 4):
                    total = total + fields[f, s] * masks[i, j, s]
                held[f, 1 + 4 * i : 5 + 4 * i, 1 + 4 * j : 5 + 4 * j] = total.reshape(
                    4, 4, 8, LANES
                )

    pl.semaphore_wait(barrier, greeted + sum(group[2] - 1 for group in groups))

    def halo_copy(buf, phase, number):
        dx, dy = DIRECTIONS[number]
        return pltpu.make_async_remote_copy(
            src_ref=buf.at[:, source_range(dx), source_range(dy)],
            dst_ref=buf.at[:, landing_range(dx), landing_range(dy)],
            send_sem=halo_send.at[phase, number],
            recv_sem=halo_recv.at[phase, number],
            device_id=at_step(dx, dy),
            device_id_type=MESH,
        )

    def halo_start(buf, phase):
        for number, (dx, dy) in enumerate(DIRECTIONS):

            @pl.when(exists(dx, dy))
            def _(number=number):
                halo_copy(buf, phase, number).start()

    def halo_arrive(buf, phase):
        for number, (dx, dy) in enumerate(DIRECTIONS):

            @pl.when(exists(-dx, -dy))
            def _(number=number):
                halo_copy(buf, phase, number).wait_recv()

    def halo_sent(buf, phase):
        for number, (dx, dy) in enumerate(DIRECTIONS):

            @pl.when(exists(dx, dy))
            def _(number=number):
                halo_copy(buf, phase, number).wait_send()

    halo_start(held, 0)

    raw[...] = jnp.zeros_like(raw)

    def load_raw(n):
        loads[n].wait()
        for t in range(TAPS):
            raw[n, t * LANES : t * LANES + 96, 0:96] = w_here[n, t]

    def widen(n, wide):
        for block, t in enumerate(HOSTS):
            at = block * LANES
            wide[at : at + LANES, :] = raw[n, t * LANES : (t + 1) * LANES, :]
            if rider(block):
                extra, third = rider(block)
                rows = extra * LANES + third * 32
                wide[at + 96 : at + LANES, :] = raw[n, rows : rows + 32, :]

    def flip(n, turned):
        turns = {}
        for t in range(TAPS):
            rows = (TAPS - 1 - t) * LANES
            turns[t] = raw[n, rows : rows + LANES, :].astype(F32).T.astype(BF16)
        for block, t in enumerate(HOSTS):
            at = block * LANES
            turned[at : at + LANES, :] = turns[t]
            if rider(block):
                extra, third = rider(block)
                turned[at + 96 : at + LANES, :] = turns[extra][third * 32 : third * 32 + 32]

    load_raw(0)
    widen(0, wm_one)
    load_raw(1)
    flip(1, wt_two)
    gain = small[0:1, :]
    bias = small[1:2, :]
    red_a[...] = jnp.zeros_like(red_a)
    red_b[...] = jnp.zeros_like(red_b)

    def columns(buf, f, cols):
        values = buf[f].reshape(100, 8, LANES)
        shifted[1] = values.reshape(10, 10, 8, LANES)
        shifted[0] = jnp.where(z_index == 0, 0.0, pltpu.roll(values, 1, 1)).reshape(
            10, 10, 8, LANES
        )
        shifted[2] = jnp.where(z_index == 7, 0.0, pltpu.roll(values, 7, 1)).reshape(
            10, 10, 8, LANES
        )
        for third in range(3):
            turned = pltpu.roll(values, 96 - 32 * third, 2)
            shifted[3 + third] = jnp.where(lane_index >= 96, turned, 0.0).reshape(
                10, 10, 8, LANES
            )

        def window(u, version):
            b = u // 3 % 3
            return shifted[version, :, b : b + 8].reshape(640, LANES)

        for block, u in enumerate(PLANE_HOSTS):
            values = window(u, u % 3)
            if rider(block):
                values = values + window(rider(block)[0], 3 + rider(block)[1])
            cols[:, block * LANES : (block + 1) * LANES] = values.astype(BF16)

    def dense_mask():
        rows = []
        for i in range(2):
            line = jnp.concatenate(
                [jnp.broadcast_to(filled[i, j], (4, 8, LANES)) for j in range(2)], axis=0
            )
            rows.append(jnp.broadcast_to(line[None], (4, 8, 8, LANES)))
        return jnp.concatenate(rows, axis=0).reshape(512, LANES)

    def interior(buf, f):
        return buf[f, 1:9, 1:9].reshape(512, LANES)

    def dot(lhs, rhs):
        return jnp.dot(lhs, rhs, preferred_element_type=F32)

    def conv(cols, wide):
        total = None
        for a in range(3):
            part = dot(
                cols[64 * a : 64 * a + 512, :],
                wide[a * PLANE * LANES : (a + 1) * PLANE * LANES, :],
            )
            total = part if total is None else total + part
        return total

    def weight_sums(left, cols, red):
        left_t = left.T.astype(BF16)[0:96]
        for a in range(3):
            for n in range(0, PLANE, 2):
                last = min(n + 2, PLANE)
                product = dot(left_t, cols[64 * a : 64 * a + 512, n * LANES : last * LANES])
                for k in range(last - n):
                    red[pl.ds((a * PLANE + n + k) * 12, 12)] = product[
                        :, k * LANES : (k + 1) * LANES
                    ].reshape(12, 8, LANES)

    reds, ins, alls = (red_a, red_b), (in_a, in_b), (all_a, all_b)
    wires, lands = (wire_a, wire_b), (land_a, land_b)
    offsets = ([jnp.int32(0)], [jnp.int32(0)])
    pieces, landings, first_sem = [], [], []
    length, landing, sems = tiles, 0, 0
    narrow = [stage > 0 and group[1] > 1 for stage, group in enumerate(groups)]
    for group in groups:
        length = length // group[2]
        pieces.append(length)
        landings.append(landing)
        first_sem.append(sems)
        landing += length * (group[2] - 1)
        sems += group[2] - 1

    def scatter_copies(which, stage):
        group, piece = groups[stage], pieces[stage]
        copies = []
        for turn in range(1, group[2]):
            other = lax.rem(rank_in(group) + turn, group[2])
            sem = first_sem[stage] + turn - 1
            if narrow[stage]:
                half = piece // 2
                source = wires[which].at[pl.ds(other * half, half)]
                target = lands[which].at[pl.ds((turn - 1) * half, half)]
            else:
                source = reds[which].at[pl.ds(offsets[which][stage] + other * piece, piece)]
                target = ins[which].at[pl.ds(landings[stage] + (turn - 1) * piece, piece)]
            copies.append(
                pltpu.make_async_remote_copy(
                    src_ref=source,
                    dst_ref=target,
                    send_sem=sum_send.at[which, sem],
                    recv_sem=sum_recv.at[which, sem],
                    device_id=member(group, other),
                    device_id_type=MESH,
                )
            )
        return copies

    def gather_copies(which, stage):
        group, piece = groups[stage], pieces[stage]
        copies = []
        for turn in range(1, group[2]):
            other = lax.rem(rank_in(group) + turn, group[2])
            sem = first_sem[stage] + turn - 1
            rows = alls[which].at[pl.ds(offsets[which][stage + 1] // 2, piece // 2)]
            copies.append(
                pltpu.make_async_remote_copy(
                    src_ref=rows,
                    dst_ref=rows,
                    send_sem=all_send.at[which, sem],
                    recv_sem=all_recv.at[which, sem],
                    device_id=member(group, other),
                    device_id_type=MESH,
                )
            )
        return copies

    def forward(which, turn):
        group, piece = groups[1], pieces[1] // 2
        owner = lax.rem(rank_in(group) + group[2] - turn, group[2])
        rows = alls[which].at[pl.ds(offsets[which][1] // 2 + owner * piece, piece)]
        pair = groups[0]
        return pltpu.make_async_remote_copy(
            src_ref=rows,
            dst_ref=rows,
            send_sem=all_send.at[which, sems + turn],
            recv_sem=all_recv.at[which, sems + turn],
            device_id=member(pair, lax.rem(rank_in(pair) + 1, pair[2])),
            device_id_type=MESH,
        )

    def scatter_end(which, stage):
        group, piece = groups[stage], pieces[stage]
        for copy in scatter_copies(which, stage):
            copy.wait()
        keep = offsets[which][stage] + rank_in(group) * piece
        offsets[which].append(keep)
        total = reds[which][pl.ds(keep, piece)]
        for turn in range(group[2] - 1):
            if narrow[stage]:
                half = piece // 2
                came = lands[which][pl.ds(turn * half, half)].astype(F32)
                total = total + came.reshape(piece, 8, LANES)
            else:
                total = total + ins[which][pl.ds(landings[stage] + turn * piece, piece)]
        if stage < stages - 1:
            reds[which][pl.ds(keep, piece)] = total
            if narrow[stage + 1]:
                wires[which][...] = total.reshape(piece // 2, 16, LANES).astype(BF16)
            return
        total = total * scale
        if which == 1:
            rest = total - total.astype(BF16).astype(F32)
            tile = lax.broadcasted_iota(jnp.int32, total.shape, 0) + keep
            row = lax.broadcasted_iota(jnp.int32, total.shape, 1)
            mine = jnp.logical_and(tile == BLOCKS * 12, jnp.logical_and(row >= 2, row < 4))
            total = jnp.where(mine, pltpu.roll(rest, 2, 1), total)
        alls[which][pl.ds(keep // 2, piece // 2)] = total.reshape(
            piece // 2, 16, LANES
        ).astype(BF16)

    def advance(which, step):
        if stages == 3 and step > 4:
            if step == 5:
                for number, copy in enumerate(gather_copies(which, 1)):
                    copy.wait()
                    forward(which, number + 1).start()
            else:
                for turn in range(groups[1][2]):
                    forward(which, turn).wait()
            return
        if step > 0:
            if step <= stages:
                scatter_end(which, step - 1)
            else:
                for copy in gather_copies(which, 2 * stages - step):
                    copy.wait()
        if step < stages:
            copies = scatter_copies(which, step)
        elif step < 2 * stages:
            copies = gather_copies(which, 2 * stages - 1 - step)
        else:
            copies = []
        for copy in copies:
            copy.start()
        if stages == 3 and step == 4:
            forward(which, 0).start()

    halo_arrive(held, 0)
    occupied = dense_mask()
    columns(held, 0, cols_a)
    first_conv = conv(cols_a, wm_one) * occupied
    pre = first_conv * gain + bias
    sigmoid = 1.0 / (1.0 + jnp.exp(-pre))
    hidden = occupied * (pre * sigmoid)
    held_two[0, 1:9, 1:9] = hidden.reshape(8, 8, 8, LANES)
    columns(held, 1, cols_b)
    weight_sums(hidden, cols_b, red_a)
    advance(0, 0)
    back_hidden = conv(cols_b, wt_two) * occupied
    back_pre = back_hidden * (sigmoid * (1.0 + pre * (1.0 - sigmoid)))
    held_two[1, 1:9, 1:9] = (back_pre * gain).reshape(8, 8, 8, LANES)
    halo_start(held_two, 1)
    red_b[BLOCKS * 12, 0:1, :] = jnp.sum(back_pre * first_conv, axis=0, keepdims=True)
    red_b[BLOCKS * 12, 1:2, :] = jnp.sum(back_pre, axis=0, keepdims=True)

    advance(0, 1)
    weight_sums(interior(held_two, 1), cols_a, red_b)
    advance(1, 0)
    flip(0, wt_one)
    advance(1, 1)
    advance(0, 2)
    halo_arrive(held_two, 1)
    columns(held_two, 1, cols_a)

    def to_slots(dense, ref):
        dense = dense.reshape(8, 8, 8, LANES)
        for s in range(4):
            total = None
            for i in range(2):
                for j in range(2):
                    part = dense[4 * i : 4 * i + 4, 4 * j : 4 * j + 4].reshape(16, 8, LANES)
                    part = part * masks[i, j, s]
                    total = part if total is None else total + part
            ref[s] = (total + pltpu.roll(total, 4, 1))[:, 0:4, 0:96]

    to_slots(interior(held, 1) + conv(cols_a, wt_one), grad_out)
    widen(1, wm_two)
    columns(held_two, 0, cols_b)
    advance(1, 2)
    second_conv = conv(cols_b, wm_two)
    advance(0, 3)
    to_slots(interior(held, 0) + second_conv, out)
    advance(0, 4)
    advance(1, 3)
    advance(1, 4)
    for step in range(5, 2 * stages + 1):
        advance(0, step)
    for block, t in enumerate(HOSTS):
        values = all_a[pl.ds(block * 6, 6)].astype(F32).reshape(96, LANES)
        gw_two[TAPS - 1 - t] = values[:, 0:96]
        if rider(block):
            extra, third = rider(block)
            lanes = slice(third * 32, third * 32 + 32)
            gw_two[TAPS - 1 - extra, :, lanes] = pltpu.roll(values, third * 32 + 32, 1)[:, lanes]
    for step in range(5, 2 * stages + 1):
        advance(1, step)
    for block, t in enumerate(HOSTS):
        values = all_b[pl.ds(block * 6, 6)].astype(F32).reshape(96, LANES).T
        gw_one[t] = values[0:96, :]
        if rider(block):
            extra, third = rider(block)
            gw_one[extra, third * 32 : third * 32 + 32, :] = values[96:LANES, :]
    last = all_b[BLOCKS * 6].astype(F32)
    last = last + pltpu.roll(last, 14, 0)
    gg_out[...] = last[0:1, 0:96]
    gb_out[...] = last[1:2, 0:96]
    halo_sent(held, 0)
    halo_sent(held_two, 1)


def body(features, cotangent, brick_slot, weight_one, weight_two, gain, bias):
    count_slots = features.shape[2]
    channels = gain.shape[0]
    size_x, size_y = lax.axis_size("gx"), lax.axis_size("gy")
    devices = size_x * size_y
    scale = 1.0 / math.sqrt(devices * count_slots * 64)
    tiles = -(-(BLOCKS * 12 + 1) // (2 * devices)) * 2 * devices
    copies = sum(group[2] - 1 for group in sum_groups(size_x, size_y))
    fields = jnp.stack([features, cotangent]).reshape(2, count_slots, 16, 4, channels)
    fields = jnp.concatenate([fields, fields], axis=3).astype(F32)
    fields = jnp.pad(fields, ((0, 0), (0, 0), (0, 0), (0, 0), (0, LANES - channels)))
    spare = ((0, 0), (0, LANES - channels))
    small = jnp.concatenate(
        [
            jnp.pad(gain.reshape(1, channels), spare),
            jnp.pad(bias.reshape(1, channels), spare),
            jnp.zeros((6, LANES), F32),
            jnp.broadcast_to(brick_slot.reshape(8, 1).astype(F32), (8, LANES)),
        ]
    )
    vmem = pl.BlockSpec(memory_space=pltpu.VMEM)
    hbm = pl.BlockSpec(memory_space=pltpu.HBM)
    slot_shape = jax.ShapeDtypeStruct((count_slots, 16, 4, channels), F32)
    weight_shape = jax.ShapeDtypeStruct((TAPS, channels, channels), F32)
    row_shape = jax.ShapeDtypeStruct((1, channels), F32)
    out, grad_features, gw_one, gw_two, gg, gb = pl.pallas_call(
        functools.partial(kernel, size_x, size_y, tiles, scale),
        out_shape=(slot_shape, slot_shape, weight_shape, weight_shape, row_shape, row_shape),
        in_specs=[vmem, vmem, hbm, hbm],
        out_specs=(vmem,) * 6,
        scratch_shapes=[
            pltpu.VMEM((2, 10, 10, 8, LANES), F32),
            pltpu.VMEM((2, 10, 10, 8, LANES), F32),
            pltpu.VMEM((6, 10, 10, 8, LANES), F32),
            pltpu.VMEM((640, PLANE * LANES), BF16),
            pltpu.VMEM((640, PLANE * LANES), BF16),
            pltpu.VMEM((BLOCKS * LANES, LANES), BF16),
            pltpu.VMEM((BLOCKS * LANES, LANES), BF16),
            pltpu.VMEM((BLOCKS * LANES, LANES), BF16),
            pltpu.VMEM((BLOCKS * LANES, LANES), BF16),
            pltpu.VMEM((2, TAPS * LANES, LANES), BF16),
            pltpu.VMEM((2, TAPS, channels, channels), BF16),
            pltpu.VMEM((tiles, 8, LANES), F32),
            pltpu.VMEM((tiles, 8, LANES), F32),
            pltpu.VMEM((tiles, 8, LANES), F32),
            pltpu.VMEM((tiles, 8, LANES), F32),
            pltpu.VMEM((tiles // 4, 16, LANES), BF16),
            pltpu.VMEM((tiles // 4, 16, LANES), BF16),
            pltpu.VMEM((tiles // 4, 16, LANES), BF16),
            pltpu.VMEM((tiles // 4, 16, LANES), BF16),
            pltpu.VMEM((tiles // 2, 16, LANES), BF16),
            pltpu.VMEM((tiles // 2, 16, LANES), BF16),
            pltpu.SemaphoreType.DMA((2, 8)),
            pltpu.SemaphoreType.DMA((2, 8)),
            pltpu.SemaphoreType.DMA((2, copies)),
            pltpu.SemaphoreType.DMA((2, copies)),
            pltpu.SemaphoreType.DMA((2, copies + size_x // 2)),
            pltpu.SemaphoreType.DMA((2, copies + size_x // 2)),
            pltpu.SemaphoreType.DMA((2,)),
        ],
        compiler_params=pltpu.CompilerParams(
            collective_id=0, has_side_effects=True, vmem_limit_bytes=48 * 1024 * 1024
        ),
    )(
        small,
        fields,
        weight_one,
        weight_two,
    )

    def pack(values):
        return values.astype(BF16).reshape(features.shape)

    return (
        pack(out),
        pack(grad_features),
        gw_one,
        gw_two,
        gg.reshape(channels),
        gb.reshape(channels),
    )


def solution(mesh):
    in_specs = (
        P("gx", "gy", None, None),
        P("gx", "gy", None, None),
        P("gx", "gy", None, None, None),
        P(),
        P(),
        P(),
        P(),
    )
    out_specs = (P("gx", "gy", None, None), P("gx", "gy", None, None), P(), P(), P(), P())
    return jax.shard_map(body, mesh=mesh, in_specs=in_specs, out_specs=out_specs, check_vma=False)
```
